128 devices in a mesh: loader: 32 (over x, y, core), pack: 4 (over z).
Axes of the slice: x: 4, y: 4, z: 4, core: 2. Of those that a mesh axis runs over, the one named last changes fastest.
Arguments:
- patches: bfloat16 [49152, 11, 256], P(('loader', 'pack')), may hold values from -6 to 6
- fields: int32 [49152], P(('loader', 'pack')), may hold values from 4 to 11, as said below
- route: int32 [49152], P(('loader', 'pack')), may hold values from 0 to 127, as said below
- frame: int32 [49152], P(('loader', 'pack')), may hold values from 0 to 3, as said below
- embed: bfloat16 [11, 256, 1024], replicated, may hold values from -0.109375 to 0.109375
- norm_attn: float32 [1024], replicated, may hold values from 0.5 to 1.5
- attn_in: bfloat16 [1024, 3072], P(None, 'pack')
- attn_out: bfloat16 [1024, 1024], P('pack'), may hold values from -0.1875 to 0.1875
- norm_mlp: float32 [1024], replicated, may hold values from 0.5 to 1.5
- mlp_in: bfloat16 [1024, 4096], P(None, 'pack'), may hold values from -0.1875 to 0.1875
- mlp_out: bfloat16 [4096, 1024], P('pack'), may hold values from -0.09375 to 0.09375
Outputs:
- mixed: bfloat16 [49152, 1024], P(('loader', 'pack'))
The draws below stay inside these ranges and needn't reach their ends.
Inputs may be any that keep to these rules, and one draw needn't show every extreme that they name: `route`: every device sends all its 384 tokens, at most 6 of them to one owner. Some owner receives exactly 6 tokens from every device, so 768 live slots; some owner receives none; the others receive from 0 to 6 from each device. Tokens attend only to tokens with the same owner and frame. `fields`: equal for all tokens with the same owner and frame.
All inputs are finite; a program needn't handle non-finite values.
Results may differ from the reference program's by a relative error of at most 0.01.
Values may be sent and summed in bfloat16 or wider, within the bound.
A program may use at most 128 MiB of HBM per device.

```python
import jax
import jax.numpy as jnp
from jax import lax

D = 1024
HEADS = 16
HEAD_WIDTH = 64
FF = 4096
FIELDS = 11
PATCH = 256
ROWS_DEV = 384
OWNERS = 128
MOST = 6
SLOTS = 768
TOKENS = 49152


def plan_tables(key):
    half = MOST // 2
    pairs = OWNERS // 2
    subkeys = jax.random.split(key, 7)
    order = jax.random.permutation(subkeys[0], OWNERS)
    offset = jax.random.randint(subkeys[1], (pairs,), 0, half + 1).at[0].set(half)
    load = jnp.zeros((OWNERS,), jnp.int32).at[order[0::2]].set(half + offset).at[order[1::2]].set(half - offset)
    signs = 2 * jax.random.randint(subkeys[2], (pairs,), 0, 2) - 1
    swing = jnp.where(offset < half, signs, 0)
    tilt = jnp.zeros((OWNERS,), jnp.int32).at[order[0::2]].set(swing).at[order[1::2]].set(-swing)
    source_ordering = jax.random.permutation(subkeys[3], OWNERS)
    parity = jnp.where(source_ordering < pairs, 1, -1)
    counts = load[None, :] + parity[:, None] * tilt[None, :]
    cumulative = jnp.cumsum(counts, axis=1)
    positions = jnp.arange(ROWS_DEV, dtype=jnp.int32)
    sorted_dest = jax.vmap(lambda line: jnp.searchsorted(line, positions, side='right'))(cumulative).astype(jnp.int32)
    shuffles = jax.vmap(lambda sub: jax.random.permutation(sub, ROWS_DEV))(jax.random.split(subkeys[4], OWNERS))
    route = jnp.take_along_axis(sorted_dest, shuffles, axis=1)
    onehot = (route[:, :, None] == jnp.arange(OWNERS, dtype=jnp.int32)[None, None, :]).astype(jnp.int32)
    rank = jnp.sum((jnp.cumsum(onehot, axis=1) - onehot) * onehot, axis=2).astype(jnp.int32)
    before = (jnp.cumsum(counts, axis=0) - counts).astype(jnp.int32)
    place = jnp.take_along_axis(before, route, axis=1) + rank
    length = ROWS_DEV // 2 * jax.random.randint(subkeys[5], (OWNERS,), 1, 5)
    length = length.at[order[0]].set(ROWS_DEV // 2)
    frame = (place // length[route]).astype(jnp.int32)
    table = jax.random.randint(subkeys[6], (OWNERS, 4), 4, FIELDS + 1)
    table = table.at[order[0], 0].set(FIELDS).at[order[0], 1].set(4)
    fields = table[route, frame]
    return (route.reshape(-1).astype(jnp.int32), frame.reshape(-1), fields.reshape(-1).astype(jnp.int32))


def draw_route(key, part):
    return plan_tables(key)[0]


def draw_frame(key, part):
    return plan_tables(key)[1]


def draw_fields(key, part):
    return plan_tables(key)[2]


def draw_attn_in(key, part):
    key = jax.random.fold_in(key, 11)
    first = jax.random.fold_in(key, 0)
    base = jax.random.normal(first, (D, HEADS, 3, HEAD_WIDTH), jnp.float32) * D ** (-0.5)
    return base.reshape(D, 3 * D).astype(jnp.bfloat16)


def levels(rng, dims, pieces, least, largest):
    factor_of = 1.0
    for axis_at, parts in pieces:
        steps = jax.random.uniform(jax.random.fold_in(jax.random.fold_in(rng, 6), axis_at), (parts,), jnp.float32, least / len(pieces), largest / len(pieces))
        factor_of = factor_of * jnp.repeat(jnp.exp(steps), dims[axis_at] // parts).reshape((-1,) + (1,) * (len(dims) - 1 - axis_at))
    return factor_of


def centred(key, extent, scale, most, cuts=(), kind=jnp.bfloat16):
    level = levels(key, extent, cuts, -0.22, 0.18) if cuts else 1.0
    values = jax.random.normal(key, extent, jnp.float32) * scale * level
    return jnp.minimum(jnp.maximum(values, -most), most).astype(kind)


def setup_inputs(seed: int = 0) -> dict:
    arg_keys = jax.random.split(jax.random.key(seed), 12)
    return {
        "patches": centred(arg_keys[0], (TOKENS, FIELDS, PATCH), 1.0, 6.0, ((0, 128),)),
        "fields": draw_fields(jax.random.fold_in(arg_keys[11], 71), 0),
        "route": draw_route(jax.random.fold_in(arg_keys[11], 71), 0),
        "frame": draw_frame(jax.random.fold_in(arg_keys[11], 71), 0),
        "embed": centred(arg_keys[4], (FIELDS, PATCH, D), (FIELDS * PATCH) ** -0.5, 0.109375),
        "norm_attn": jnp.clip(1.0 + 0.1 * jax.random.normal(arg_keys[5], (D,), jnp.float32), 0.5, 1.5),
        "attn_in": draw_attn_in(jax.random.fold_in(arg_keys[11], 71), 0),
        "attn_out": centred(arg_keys[7], (D, D), D ** -0.5, 0.1875, ((0, 4),)),
        "norm_mlp": jnp.clip(1.0 + 0.1 * jax.random.normal(arg_keys[8], (D,), jnp.float32), 0.5, 1.5),
        "mlp_in": centred(arg_keys[9], (D, FF), D ** -0.5, 0.1875, ((1, 4),)),
        "mlp_out": centred(arg_keys[10], (FF, D), FF ** -0.5, 0.09375, ((0, 4),)),
    }


def rms_norm(values, gain):
    mean_square = lax.optimization_barrier(jnp.mean(values * values, axis=-1, keepdims=True))
    return values * lax.rsqrt(mean_square + 1e-06) * gain

def attend(qkv, tags):
    same = tags[:, :, None] == tags[:, None, :]
    heads = jnp.moveaxis(qkv, 2, 0)

    def one_head(part):
        query_rows = part[:, :, 0].astype(jnp.float32)
        key_rows = part[:, :, 1].astype(jnp.float32)
        value_rows = part[:, :, 2].astype(jnp.float32)
        logit_scores = jnp.einsum('ecl,enl->ecn', query_rows, key_rows) * HEAD_WIDTH ** (-0.5)
        logit_scores = jnp.where(same, logit_scores, -1e+30)
        highest = lax.optimization_barrier(jnp.max(logit_scores, axis=-1, keepdims=True))
        shifted = jnp.exp(logit_scores - highest)
        attention_weight = (shifted / lax.optimization_barrier(jnp.sum(shifted, axis=-1, keepdims=True))).astype(jnp.bfloat16)
        return jnp.einsum('ivn,inf->ivf', attention_weight.astype(jnp.float32), value_rows).astype(jnp.bfloat16)
    result = lax.map(one_head, heads)
    result = jnp.moveaxis(result, 0, 2)
    return result.reshape(result.shape[0], result.shape[1], -1)

def owner_layer(owner_rows, owner_tags, norm_attn, attn_in, attn_out, norm_mlp, mlp_in, mlp_out):
    slot_count = owner_rows.shape[0]
    residual = owner_rows.astype(jnp.float32)
    normed = rms_norm(residual, norm_attn).astype(jnp.bfloat16)
    qkv = jnp.dot(normed, attn_in, preferred_element_type=jnp.float32).astype(jnp.bfloat16)
    qkv = qkv.reshape(1, slot_count, HEADS, 3, HEAD_WIDTH)
    heads_out = attend(qkv, owner_tags[None, :])[0]
    hidden_state = residual + jnp.dot(heads_out, attn_out, preferred_element_type=jnp.float32)
    normed_mlp = rms_norm(hidden_state, norm_mlp).astype(jnp.bfloat16)
    inner = jax.nn.gelu(jnp.dot(normed_mlp, mlp_in, preferred_element_type=jnp.float32)).astype(jnp.bfloat16)
    return (hidden_state + jnp.dot(inner, mlp_out, preferred_element_type=jnp.float32)).astype(jnp.bfloat16)

def reference(patches, fields, route, frame, embed, norm_attn, attn_in, attn_out, norm_mlp, mlp_in, mlp_out):
    live = jnp.arange(FIELDS, dtype=jnp.int32)[None, :] < fields[:, None]
    flat = jnp.where(live[:, :, None], patches, jnp.zeros_like(patches)).reshape(TOKENS, FIELDS * PATCH)
    embedded = jnp.dot(flat, embed.reshape(FIELDS * PATCH, D), preferred_element_type=jnp.float32).astype(jnp.bfloat16)
    by_source = route.reshape(OWNERS, ROWS_DEV)
    onehot = (by_source[:, :, None] == jnp.arange(OWNERS, dtype=jnp.int32)[None, None, :]).astype(jnp.int32)
    before = (jnp.cumsum(onehot, axis=1) - onehot).astype(jnp.int32)
    rank = lax.optimization_barrier(jnp.sum(before * onehot, axis=2)).astype(jnp.int32)
    source = jnp.arange(OWNERS, dtype=jnp.int32)[:, None]
    target = (by_source * SLOTS + source * MOST + rank).reshape(TOKENS).astype(jnp.int32)
    buffer = jnp.zeros((OWNERS * SLOTS, D), jnp.bfloat16).at[target].set(embedded)
    tagged_tokens = jnp.full((OWNERS * SLOTS,), -1, jnp.int32).at[target].set(frame.astype(jnp.int32))

    def one_owner(pair):
        return owner_layer(pair[0], pair[1], norm_attn, attn_in, attn_out, norm_mlp, mlp_in, mlp_out)
    outputs = lax.map(one_owner, (buffer.reshape(OWNERS, SLOTS, D), tagged_tokens.reshape(OWNERS, SLOTS)))
    return outputs.reshape(OWNERS * SLOTS, D)[target]
```

```python
import functools

import jax
import jax.numpy as jnp
from jax import lax
from jax.experimental import pallas as pl
from jax.experimental.pallas import tpu as pltpu
from jax.sharding import PartitionSpec as P

D = 1024
FIELDS = 11
PATCH = 256
ROWS = 384
OWNERS = 128
MOST = 6
SLOTS = 768
CHUNKS = D // 128
NB_OUT = 56
NB_BACK = 48
EPS = 1e-06
BIG = 1e30
EXP_SCALE = 1.4426950408889634 / 8.0
MESH = pl.DeviceIdType.MESH
F32 = jnp.float32
BF16 = jnp.bfloat16

PER_WEIGHT = 19


def device(x, y, c, z):
    return (((x % 4) * 4 + y % 4) * 2 + c % 2, z % 4)


def dot(a, b):
    return jnp.dot(a, b, preferred_element_type=F32)


def iota(shape, dim):
    return lax.broadcasted_iota(jnp.int32, shape, dim)


def kernel(
    patches_ref,
    embed_ref,
    route_ref,
    frame_ref,
    fields_ref,
    norm_attn_ref,
    norm_mlp_ref,
    attn_in_ref,
    attn_out_ref,
    mlp_in_ref,
    mlp_out_ref,
    out_ref,
    w_in,
    w_out,
    w_up,
    w_down,
    raw_in,
    embed_v,
    flat,
    embedded,
    stage,
    send_out,
    recv_out,
    send_back,
    recv_back,
    rows,
    normed,
    qkv,
    heads,
    hidden,
    total,
    gather,
    local_sem,
    row_sem,
    wsend,
    wrecv,
):
    loader = lax.axis_index("loader")
    z = lax.axis_index("pack")
    x, y, c = loader // 8, (loader // 2) % 4, loader % 2
    me = loader * 4 + z
    r = jnp.where(c == 0, x, y)

    loads = []

    def load(src, dst):
        copy = pltpu.make_async_copy(src, dst, local_sem.at[len(loads)])
        copy.start()
        loads.append(copy)
        return copy

    get_in = load(attn_in_ref, raw_in)
    get_embed = load(embed_ref, embed_v)
    get_patches = load(patches_ref, flat)
    get_out = load(attn_out_ref, w_out.at[z])
    get_up = load(mlp_in_ref, w_up.at[z])
    get_down = load(mlp_out_ref, w_down.at[z])

    def peer(k):
        dc, dx, dy, dz = k % 2, (k // 2) % 4, (k // 8) % 4, k // 32
        px, py, pc, pz = (x + dx) % 4, (y + dy) % 4, (c + dc) % 2, (z + dz) % 4
        to = (px * 4 + py) * 2 + pc
        return (to, pz), to * 4 + pz

    barrier = pltpu.get_barrier_semaphore()

    def greet(k, carry):
        pl.semaphore_signal(barrier, inc=1, device_id=peer(k)[0], device_id_type=MESH)
        return carry

    lax.fori_loop(1, OWNERS, greet, 0)

    get_in.wait()

    def reorder(n, carry):
        col = iota((768, 256), 1)
        source = (col >> 6) * 192 + n * 64 + (col & 63)
        pick = (iota((768, 256), 0) == source).astype(BF16)
        at = pl.multiple_of(n * 256, 256)
        w_in[z, :, pl.ds(at, 256)] = dot(raw_in[...], pick).astype(BF16)
        return carry

    lax.fori_loop(0, 3, reorder, 0)

    route_row = route_ref[...]
    frame_row = frame_ref[...].astype(F32)
    eye = iota((ROWS, ROWS), 0) == iota((ROWS, ROWS), 1)

    def column(row):
        return jnp.sum(jnp.where(eye, row, 0.0), axis=1, keepdims=True)

    onehot = (iota((OWNERS, ROWS), 0) == route_row).astype(F32)
    before = (iota((ROWS, ROWS), 0) < iota((ROWS, ROWS), 1)).astype(BF16)
    rank_row = jnp.sum(dot(onehot.astype(BF16), before) * onehot, axis=0, keepdims=True)
    route_col = column(route_row.astype(F32))
    rank_col = column(rank_row)
    fields_col = column(fields_ref[...].astype(F32))
    owner_lane = iota((ROWS, OWNERS), 1).astype(F32)
    for k in range(MOST):
        gather[:, k * OWNERS : (k + 1) * OWNERS] = (
            (owner_lane == route_col) & (rank_col == float(k))
        ).astype(BF16)

    get_embed.wait()
    get_patches.wait()
    for f in range(FIELDS):
        part = flat[f]
        flat[f] = jnp.where(fields_col > float(f), part.astype(F32), 0.0).astype(BF16)

    def embed_tile(n, carry):
        at = pl.multiple_of(n * 256, 256)
        acc = dot(flat[0], embed_v[0, :, pl.ds(at, 256)])
        for f in range(1, FIELDS):
            acc = acc + dot(flat[f], embed_v[f, :, pl.ds(at, 256)])
        embedded[:, pl.ds(at, 256)] = acc.astype(BF16)
        return carry

    lax.fori_loop(0, 4, embed_tile, 0)

    for k in range(MOST):
        place = onehot * (rank_row == float(k)).astype(F32)
        tag = jnp.sum(place * (frame_row + 1.0), axis=1, keepdims=True) - 1.0
        placed = dot(place.astype(BF16), embedded[...])
        for n in range(CHUNKS):
            stage[pl.ds(k * CHUNKS + n, OWNERS, stride=NB_OUT), :] = placed[
                :, n * 128 : (n + 1) * 128
            ]
        stage[pl.ds(48 + k, OWNERS, stride=NB_OUT), :] = jnp.broadcast_to(tag, (OWNERS, 128))
    for k in range(48 + MOST, NB_OUT):
        stage[pl.ds(k, OWNERS, stride=NB_OUT), :] = jnp.zeros((OWNERS, 128), F32)

    def pack_out(k, carry):
        at = pl.multiple_of(k * 8 * NB_OUT, 8 * NB_OUT)
        block = stage[pl.ds(at, 8 * NB_OUT), :]
        send_out[pl.ds(k * 8, 8)] = block.reshape(8, NB_OUT, 128).astype(BF16)
        return carry

    lax.fori_loop(0, OWNERS // 8, pack_out, 0)

    get_out.wait()
    get_up.wait()
    get_down.wait()
    pl.semaphore_wait(barrier, OWNERS - 1)

    weights = (w_in, w_out, w_up, w_down)
    copies = {}

    def send(w, slot, block, to):
        copy = pltpu.make_async_remote_copy(
            block,
            block,
            wsend.at[w * PER_WEIGHT + slot],
            wrecv.at[w * PER_WEIGHT + slot],
            device_id=to,
            device_id_type=MESH,
        )
        copy.start()
        copies[w, slot] = copy

    def arrived(w, slot):
        copies[w, slot].wait_recv()

    z_of = ((z + 3) % 4, (z + 1) % 4, (z + 2) % 4)
    up_z, down_z = device(x, y, c, z + 1), device(x, y, c, z + 3)
    one = jnp.where(c == 0, 1, 0)
    up_r = device(x + one, y + 1 - one, c, z)
    down_r = device(x + 3 * one, y + 3 - 3 * one, c, z)
    other = device(x, y, c + 1, z)

    def part(w, which, q, half=None):
        size = weights[w].shape[1] // 8
        start = (c * 4 + q % 4) * size
        if half is not None:
            size = size // 2
            start = start + half * size
        return weights[w].at[which, pl.ds(pl.multiple_of(start, size), size)]

    def begin(w):
        send(w, 0, part(w, z, r), up_z)
        send(w, 1, part(w, z, r), down_z)

    def ring(w, i):
        send(w, 4 + 4 * i, part(w, z_of[i], r), up_r)
        send(w, 5 + 4 * i, part(w, z_of[i], r), down_r)

    def near(w):
        arrived(w, 0)
        send(w, 2, part(w, z_of[0], r, 0), up_z)
        ring(w, 0)
        arrived(w, 1)
        send(w, 3, part(w, z_of[1], r, 1), down_z)
        ring(w, 1)

    def far(w):
        arrived(w, 2)
        arrived(w, 3)
        ring(w, 2)

    def onward(w, i):
        arrived(w, 4 + 4 * i)
        send(w, 6 + 4 * i, part(w, z_of[i], r + 3, 0), up_r)
        arrived(w, 5 + 4 * i)
        send(w, 7 + 4 * i, part(w, z_of[i], r + 1, 1), down_r)

    def share(w, i):
        arrived(w, 6 + 4 * i)
        arrived(w, 7 + 4 * i)
        size = weights[w].shape[1] // 2
        at = pl.multiple_of(c * size, size)
        send(w, 16 + i, weights[w].at[z_of[i], pl.ds(at, size)], other)

    def ready(w, i):
        arrived(w, 16 + i)

    def exchange(source, target, sems):
        own = pltpu.make_async_copy(source.at[me], target.at[me], sems[2])
        own.start()

        def one_peer(k, carry):
            to, index = peer(k)
            pltpu.make_async_remote_copy(
                source.at[index],
                target.at[me],
                sems[0],
                sems[1],
                device_id=to,
                device_id_type=MESH,
            ).start()
            return carry

        lax.fori_loop(1, OWNERS, one_peer, 0)
        return own

    def finish(source, target, sems, own):
        own.wait()
        pltpu.make_async_remote_copy(
            source.at[pl.ds(0, OWNERS - 1)],
            target.at[pl.ds(0, OWNERS - 1)],
            sems[0],
            sems[1],
            device_id=other,
            device_id_type=MESH,
        ).wait()

    sems_out = (row_sem.at[0], row_sem.at[1], row_sem.at[2])
    sems_back = (row_sem.at[3], row_sem.at[4], row_sem.at[5])

    begin(0)
    own_out = exchange(send_out, recv_out, sems_out)
    begin(1)
    begin(2)
    begin(3)
    near(0)
    far(0)
    near(1)
    onward(0, 0)
    onward(0, 1)
    onward(0, 2)
    near(2)
    share(0, 0)
    share(0, 1)
    share(0, 2)
    near(3)
    far(1)
    finish(send_out, recv_out, sems_out, own_out)

    def unpack_out(k, carry):
        at = pl.multiple_of(k * 8 * NB_OUT, 8 * NB_OUT)
        block = recv_out[pl.ds(k * 8, 8)].astype(F32)
        stage[pl.ds(at, 8 * NB_OUT), :] = block.reshape(8 * NB_OUT, 128)
        return carry

    lax.fori_loop(0, OWNERS // 8, unpack_out, 0)

    def norm_rows(k, carry):
        at = pl.multiple_of(k * OWNERS, OWNERS)
        square = jnp.zeros((OWNERS, 128), F32)
        for n in range(CHUNKS):
            part_rows = stage[pl.ds(k * CHUNKS + n, OWNERS, stride=NB_OUT), :]
            rows[pl.ds(at, OWNERS), n * 128 : (n + 1) * 128] = part_rows
            square = square + part_rows * part_rows
        mean = jnp.sum(square, axis=1, keepdims=True) * (1.0 / D)
        scaled = rows[pl.ds(at, OWNERS), :] * lax.rsqrt(mean + EPS) * norm_attn_ref[...]
        normed[pl.ds(at, OWNERS), :] = scaled.astype(BF16)
        return carry

    for k in range(MOST):
        norm_rows(k, 0)

    tags = jnp.concatenate(
        [stage[pl.ds(48 + k, OWNERS, stride=NB_OUT), :] for k in range(MOST)], axis=0
    )
    lane = iota((SLOTS, 128), 1)
    low = lane < 64
    same_tag = tags == ((lane & 63) - 1).astype(F32)
    tag_query = same_tag.astype(BF16)
    tag_key = jnp.where(same_tag | ((lane & 63) > 4), 0.0, -BIG).astype(BF16)

    def attend(which):
        def project(n, carry):
            at = pl.multiple_of(n * 256, 256)
            qkv[:, pl.ds(at, 256)] = dot(normed[...], w_in[which, :, pl.ds(at, 256)]).astype(BF16)
            return carry

        lax.fori_loop(0, 3, project, 0)

        def pair(p, carry):
            at = pl.multiple_of(p * 128, 128)
            query = qkv[:, pl.ds(at, 128)]
            key = qkv[:, pl.ds(at + 256, 128)]
            value = qkv[:, pl.ds(at + 512, 128)]
            results = []
            for h in range(2):
                mine = low if h == 0 else jnp.logical_not(low)
                keys = jnp.where(mine, key, tag_key)
                values = jnp.where(mine, value, jnp.ones_like(value))
                queries = jnp.where(mine, query, tag_query)
                blocks = []
                for b in range(3):
                    scores = lax.dot_general(
                        queries[b * 256 : (b + 1) * 256],
                        keys,
                        (((1,), (1,)), ((), ())),
                        preferred_element_type=F32,
                    )
                    highest = jnp.max(scores, axis=1, keepdims=True)
                    shifted = jnp.exp2((scores - highest) * EXP_SCALE).astype(BF16)
                    blocks.append(dot(shifted, values))
                results.append(blocks)
            for b in range(3):
                half = low[:256]
                top = jnp.where(half, results[0][b], results[1][b])
                sums = jnp.where(half, results[1][b], results[0][b])
                heads[which * 2 + p, b * 256 : (b + 1) * 256, :] = top / pltpu.roll(sums, 64, 1)
            return carry

        lax.fori_loop(0, 2, pair, 0)

    attend(z)
    far(2)
    onward(1, 0)
    onward(1, 1)
    onward(1, 2)
    ready(0, 0)
    attend(z_of[0])
    far(3)
    onward(2, 0)
    onward(2, 1)
    share(1, 0)
    share(1, 1)
    share(1, 2)
    ready(0, 1)
    attend(z_of[1])
    onward(2, 2)
    onward(3, 0)
    share(2, 0)
    share(2, 1)
    ready(0, 2)
    attend(z_of[2])

    for k in range(MOST):
        for n in range(CHUNKS):
            stage[pl.ds(k * CHUNKS + n, OWNERS, stride=NB_BACK), :] = heads[
                n, k * OWNERS : (k + 1) * OWNERS, :
            ]

    def pack_back(k, carry):
        at = pl.multiple_of(k * 8 * NB_BACK, 8 * NB_BACK)
        block = stage[pl.ds(at, 8 * NB_BACK), :]
        send_back[pl.ds(k * 8, 8)] = block.reshape(8, NB_BACK, 128).astype(BF16)
        return carry

    lax.fori_loop(0, OWNERS // 8, pack_back, 0)
    own_back = exchange(send_back, recv_back, sems_back)
    onward(3, 1)
    onward(3, 2)
    share(2, 2)
    share(3, 0)
    share(3, 1)
    share(3, 2)
    for i in range(3):
        ready(1, i)
    finish(send_back, recv_back, sems_back, own_back)

    def unpack_back(k, carry):
        at = pl.multiple_of(k * 8 * NB_BACK, 8 * NB_BACK)
        block = recv_back[pl.ds(k * 8, 8)].astype(F32)
        stage[pl.ds(at, 8 * NB_BACK), :] = block.reshape(8 * NB_BACK, 128)
        return carry

    lax.fori_loop(0, OWNERS // 8, unpack_back, 0)
    for k in range(MOST):
        for n in range(CHUNKS):
            normed[k * OWNERS : (k + 1) * OWNERS, n * 128 : (n + 1) * 128] = stage[
                pl.ds(k * CHUNKS + n, OWNERS, stride=NB_BACK), :
            ].astype(BF16)

    def take(n, carry):
        at = pl.multiple_of(n * 256, 256)
        qkv[0:ROWS, pl.ds(0, 256)] = dot(gather[...], normed[:, pl.ds(at, 256)]).astype(BF16)
        partial = qkv[0:ROWS, pl.ds(0, 256)]
        for m in range(4):
            to = slice(m * 256, (m + 1) * 256)
            hidden[:, to] = hidden[:, to] + dot(partial, w_out[n, :, to])
        return carry

    hidden[...] = embedded[...].astype(F32)
    lax.fori_loop(0, 4, take, 0)
    values = hidden[...]
    mean = jnp.sum(values * values, axis=1, keepdims=True) * (1.0 / D)
    normed[0:ROWS, :] = (values * lax.rsqrt(mean + EPS) * norm_mlp_ref[...]).astype(BF16)
    total[...] = hidden[...]

    def mlp(which):
        def widen(n, carry):
            at = pl.multiple_of(n * 256, 256)
            up = dot(normed[0:ROWS, :], w_up[which, :, pl.ds(at, 256)])
            normed[ROWS:SLOTS, pl.ds(at, 256)] = jax.nn.gelu(up).astype(BF16)
            return carry

        lax.fori_loop(0, 4, widen, 0)

        def narrow(n, carry):
            at = pl.multiple_of(n * 256, 256)
            total[:, pl.ds(at, 256)] = total[:, pl.ds(at, 256)] + dot(
                normed[ROWS:SLOTS, :], w_down[which, :, pl.ds(at, 256)]
            )
            return carry

        lax.fori_loop(0, 4, narrow, 0)

    mlp(z)
    for i in range(3):
        ready(2, i)
        ready(3, i)
        mlp(z_of[i])
    out_ref[...] = total[...].astype(BF16)
    for copy in copies.values():
        copy.wait_send()


def local(
    patches, fields, route, frame, embed, norm_attn, attn_in, attn_out, norm_mlp, mlp_in, mlp_out
):
    by_field = jnp.transpose(patches, (1, 0, 2))
    whole = pl.BlockSpec(memory_space=pl.ANY)
    vmem = pl.BlockSpec(memory_space=pltpu.VMEM)
    return pl.pallas_call(
        kernel,
        out_shape=jax.ShapeDtypeStruct((ROWS, D), BF16),
        in_specs=[whole, whole, vmem, vmem, vmem, vmem, vmem, whole, whole, whole, whole],
        out_specs=vmem,
        scratch_shapes=[
            pltpu.VMEM((4, D, 768), BF16),
            pltpu.VMEM((4, 256, D), BF16),
            pltpu.VMEM((4, D, D), BF16),
            pltpu.VMEM((4, D, D), BF16),
            pltpu.VMEM((D, 768), BF16),
            pltpu.VMEM((FIELDS, PATCH, D), BF16),
            pltpu.VMEM((FIELDS, ROWS, PATCH), BF16),
            pltpu.VMEM((ROWS, D), BF16),
            pltpu.VMEM((OWNERS * NB_OUT, 128), F32),
            pltpu.VMEM((OWNERS, NB_OUT, 128), BF16),
            pltpu.VMEM((OWNERS, NB_OUT, 128), BF16),
            pltpu.VMEM((OWNERS, NB_BACK, 128), BF16),
            pltpu.VMEM((OWNERS, NB_BACK, 128), BF16),
            pltpu.VMEM((SLOTS, D), F32),
            pltpu.VMEM((SLOTS, D), BF16),
            pltpu.VMEM((SLOTS, 768), BF16),
            pltpu.VMEM((CHUNKS, SLOTS, 128), F32),
            pltpu.VMEM((ROWS, D), F32),
            pltpu.VMEM((ROWS, D), F32),
            pltpu.VMEM((ROWS, SLOTS), BF16),
            pltpu.SemaphoreType.DMA((6,)),
            pltpu.SemaphoreType.DMA((6,)),
            pltpu.SemaphoreType.DMA((4 * PER_WEIGHT,)),
            pltpu.SemaphoreType.DMA((4 * PER_WEIGHT,)),
        ],
        compiler_params=pltpu.CompilerParams(
            collective_id=0, has_side_effects=True, vmem_limit_bytes=62 * 1024 * 1024
        ),
        cost_estimate=pl.CostEstimate(
            flops=25_000_000_000, bytes_accessed=16_000_000, transcendentals=11_000_000
        ),
    )(
        by_field,
        embed,
        route.reshape(1, ROWS),
        frame.reshape(1, ROWS),
        fields.reshape(1, ROWS),
        norm_attn.reshape(1, D),
        norm_mlp.reshape(1, D),
        attn_in,
        attn_out,
        mlp_in,
        mlp_out,
    )


def solution(mesh):
    return jax.shard_map(
        local,
        mesh=mesh,
        in_specs=(
            P(("loader", "pack"), None, None),
            P(("loader", "pack")),
            P(("loader", "pack")),
            P(("loader", "pack")),
            P(),
            P(),
            P(None, "pack"),
            P("pack", None),
            P(),
            P(None, "pack"),
            P("pack", None),
        ),
        out_specs=P(("loader", "pack"), None),
        check_vma=False,
    )
```

```python
import functools

import jax
import jax.numpy as jnp
from jax import lax
from jax.experimental import pallas as pl
from jax.experimental.pallas import tpu as pltpu
from jax.sharding import PartitionSpec as P

D = 1024
FIELDS = 11
PATCH = 256
ROWS = 384
OWNERS = 128
MOST = 6
SLOTS = 768
CHUNKS = D // 128
NB_OUT = 56
NB_BACK = 48
EPS = 1e-06
BIG = 1e30
EXP_SCALE = 1.4426950408889634 / 8.0
MESH = pl.DeviceIdType.MESH
F32 = jnp.float32
BF16 = jnp.bfloat16

PER_WEIGHT = 19


def device(x, y, c, z):
    return (((x % 4) * 4 + y % 4) * 2 + c % 2, z % 4)


def dot(a, b):
    return jnp.dot(a, b, preferred_element_type=F32)


def iota(shape, dim):
    return lax.broadcasted_iota(jnp.int32, shape, dim)


def kernel(
    patches_ref,
    embed_ref,
    route_ref,
    frame_ref,
    fields_ref,
    norm_attn_ref,
    norm_mlp_ref,
    attn_in_ref,
    attn_out_ref,
    mlp_in_ref,
    mlp_out_ref,
    out_ref,
    w_in,
    w_out,
    w_up,
    w_down,
    raw_in,
    embed_v,
    flat,
    embedded,
    stage,
    send_out,
    recv_out,
    send_back,
    recv_back,
    rows,
    normed,
    qkv,
    heads,
    hidden,
    total,
    gather,
    local_sem,
    row_sem,
    wsend,
    wrecv,
    here,
):
    loader = lax.axis_index("loader")
    z = lax.axis_index("pack")
    x, y, c = loader // 8, (loader // 2) % 4, loader % 2
    me = loader * 4 + z
    r = jnp.where(c == 0, x, y)

    loads = []

    def load(src, dst):
        copy = pltpu.make_async_copy(src, dst, local_sem.at[len(loads)])
        copy.start()
        loads.append(copy)
        return copy

    get_in = load(attn_in_ref, raw_in)
    get_embed = load(embed_ref, embed_v)
    get_patches = load(patches_ref, flat)
    get_out = load(attn_out_ref, w_out.at[z])
    get_up = load(mlp_in_ref, w_up.at[z])
    get_down = load(mlp_out_ref, w_down.at[z])

    def peer(k):
        dx, dc = k % 4, (k // 64 + k) % 2
        dy, dz = (k // 4 + dx) % 4, (k // 16 + 4 - dx) % 4
        px, py, pc, pz = (x + dx) % 4, (y + dy) % 4, (c + dc) % 2, (z + dz) % 4
        to = (px * 4 + py) * 2 + pc
        return (to, pz), to * 4 + pz

    barrier = pltpu.get_barrier_semaphore()
    line_x = [device(x + k, y, c, z) for k in (1, 3, 2)]
    line_y = [device(x, y + k, c, z) for k in (1, 3, 2)]
    line_z = [device(x, y, c, z + k) for k in (1, 3, 2)]
    for to in line_x + line_y + line_z + [device(x, y, c + 1, z)]:
        pl.semaphore_signal(barrier, inc=1, device_id=to, device_id_type=MESH)

    def greet(line, stage):
        for to in line:
            pl.semaphore_signal(here.at[stage], inc=1, device_id=to, device_id_type=MESH)

    def heard(stage):
        pl.semaphore_wait(here.at[stage], 3)

    get_in.wait()

    def reorder(n, carry):
        col = iota((768, 256), 1)
        source = (col >> 6) * 192 + n * 64 + (col & 63)
        pick = (iota((768, 256), 0) == source).astype(BF16)
        at = pl.multiple_of(n * 256, 256)
        w_in[z, :, pl.ds(at, 256)] = dot(raw_in[...], pick).astype(BF16)
        return carry

    lax.fori_loop(0, 3, reorder, 0)

    weights = (w_in, w_out, w_up, w_down)
    z_of = ((z + 3) % 4, (z + 1) % 4, (z + 2) % 4)
    up_z, down_z = device(x, y, c, z + 1), device(x, y, c, z + 3)
    one = jnp.where(c == 0, 1, 0)
    up_r = device(x + one, y + 1 - one, c, z)
    down_r = device(x + 3 * one, y + 3 - 3 * one, c, z)
    other = device(x, y, c + 1, z)

    def part(w, which, q, half=None):
        size = weights[w].shape[1] // 8
        start = (c * 4 + q % 4) * size
        if half is not None:
            size = size // 2
            start = start + half * size
        return weights[w].at[which, pl.ds(pl.multiple_of(start, size), size)]

    def copy_of(w, slot):
        if slot < 2:
            block, to = part(w, z, r), (up_z, down_z)[slot]
        elif slot < 4:
            block, to = part(w, z_of[slot - 2], r, slot - 2), (up_z, down_z)[slot - 2]
        elif slot < 16:
            i, step = (slot - 4) // 4, (slot - 4) % 4
            to = (up_r, down_r)[step % 2]
            if step < 2:
                block = part(w, z_of[i], r)
            else:
                block = part(w, z_of[i], r + (3 if step == 2 else 1), step - 2)
        else:
            size = weights[w].shape[1] // 2
            at = pl.multiple_of(c * size, size)
            block, to = weights[w].at[z_of[slot - 16], pl.ds(at, size)], other
        return pltpu.make_async_remote_copy(
            block,
            block,
            wsend.at[w * PER_WEIGHT + slot],
            wrecv.at[w * PER_WEIGHT + slot],
            device_id=to,
            device_id_type=MESH,
        )

    def send(w, slot):
        copy_of(w, slot).start()

    def arrived(w, slot):
        copy_of(w, slot).wait_recv()

    def begin(w):
        send(w, 0)
        send(w, 1)

    def ring(w, i):
        send(w, 4 + 4 * i)
        send(w, 5 + 4 * i)

    def near(w):
        arrived(w, 0)
        send(w, 2)
        ring(w, 0)
        arrived(w, 1)
        send(w, 3)
        ring(w, 1)

    def far(w):
        arrived(w, 2)
        arrived(w, 3)
        ring(w, 2)

    def onward(w, i):
        arrived(w, 4 + 4 * i)
        send(w, 6 + 4 * i)
        arrived(w, 5 + 4 * i)
        send(w, 7 + 4 * i)

    def share(w, i):
        arrived(w, 6 + 4 * i)
        arrived(w, 7 + 4 * i)
        send(w, 16 + i)

    def ready(w, i):
        arrived(w, 16 + i)

    pl.semaphore_wait(barrier, 10)
    begin(0)
    greet(line_z, 0)
    get_out.wait()
    begin(1)

    route_row = route_ref[...].reshape(1, ROWS)
    frame_row = frame_ref[...].reshape(1, ROWS).astype(F32)
    eye = iota((ROWS, ROWS), 0) == iota((ROWS, ROWS), 1)

    def column(row):
        return jnp.sum(jnp.where(eye, row, 0.0), axis=1, keepdims=True)

    onehot = (iota((OWNERS, ROWS), 0) == route_row).astype(F32)
    before = (iota((ROWS, ROWS), 0) < iota((ROWS, ROWS), 1)).astype(BF16)
    rank_row = jnp.sum(dot(onehot.astype(BF16), before) * onehot, axis=0, keepdims=True)
    route_col = column(route_row.astype(F32))
    rank_col = column(rank_row)
    fields_col = column(fields_ref[...].reshape(1, ROWS).astype(F32))
    owner_lane = iota((ROWS, OWNERS), 1).astype(F32)
    for k in range(MOST):
        gather[:, k * OWNERS : (k + 1) * OWNERS] = (
            (owner_lane == route_col) & (rank_col == float(k))
        ).astype(BF16)

    heard(0)
    greet(line_y, 1)

    get_embed.wait()
    get_patches.wait()
    for f in range(FIELDS):
        pixels = flat[f]
        flat[f] = jnp.where(fields_col > float(f), pixels.astype(F32), 0.0).astype(BF16)

    def embed_tile(n, carry):
        at = pl.multiple_of(n * 256, 256)
        acc = dot(flat[0], embed_v[0, :, pl.ds(at, 256)])
        for f in range(1, FIELDS):
            acc = acc + dot(flat[f], embed_v[f, :, pl.ds(at, 256)])
        embedded[:, pl.ds(at, 256)] = acc.astype(BF16)
        return carry

    lax.fori_loop(0, 4, embed_tile, 0)

    heard(1)
    greet(line_x, 2)
    near(0)

    for k in range(MOST):
        place = onehot * (rank_row == float(k)).astype(F32)
        tag = jnp.sum(place * (frame_row + 1.0), axis=1, keepdims=True) - 1.0
        placed = dot(place.astype(BF16), embedded[...])
        for n in range(CHUNKS):
            stage[pl.ds(k * CHUNKS + n, OWNERS, stride=NB_OUT), :] = placed[
                :, n * 128 : (n + 1) * 128
            ]
        stage[pl.ds(48 + k, OWNERS, stride=NB_OUT), :] = jnp.broadcast_to(tag, (OWNERS, 128))
    for k in range(48 + MOST, NB_OUT):
        stage[pl.ds(k, OWNERS, stride=NB_OUT), :] = jnp.zeros((OWNERS, 128), F32)

    def pack_out(k, carry):
        at = pl.multiple_of(k * 8 * NB_OUT, 8 * NB_OUT)
        block = stage[pl.ds(at, 8 * NB_OUT), :]
        send_out[pl.ds(k * 8, 8)] = block.reshape(8, NB_OUT, 128).astype(BF16)
        return carry

    lax.fori_loop(0, OWNERS // 8, pack_out, 0)

    heard(2)
    near(1)
    get_up.wait()
    begin(2)
    far(0)
    far(1)

    def exchange(source, target, sems):
        own = pltpu.make_async_copy(source.at[me], target.at[me], sems[2])
        own.start()

        def one_peer(k, carry):
            to, index = peer(k)
            pltpu.make_async_remote_copy(
                source.at[index],
                target.at[me],
                sems[0],
                sems[1],
                device_id=to,
                device_id_type=MESH,
            ).start()
            return carry

        lax.fori_loop(1, OWNERS, one_peer, 0)
        return own

    def finish(source, target, sems, own):
        own.wait()
        pltpu.make_async_remote_copy(
            source.at[pl.ds(0, OWNERS - 1)],
            target.at[pl.ds(0, OWNERS - 1)],
            sems[0],
            sems[1],
            device_id=other,
            device_id_type=MESH,
        ).wait()

    sems_out = (row_sem.at[0], row_sem.at[1], row_sem.at[2])
    sems_back = (row_sem.at[3], row_sem.at[4], row_sem.at[5])

    own_out = exchange(send_out, recv_out, sems_out)
    for i in range(3):
        onward(0, i)
    near(2)
    for i in range(3):
        share(0, i)
    get_down.wait()
    begin(3)
    for i in range(3):
        onward(1, i)
    far(2)
    for i in range(3):
        share(1, i)
    finish(send_out, recv_out, sems_out, own_out)

    def unpack_out(k, carry):
        at = pl.multiple_of(k * 8 * NB_OUT, 8 * NB_OUT)
        block = recv_out[pl.ds(k * 8, 8)].astype(F32)
        stage[pl.ds(at, 8 * NB_OUT), :] = block.reshape(8 * NB_OUT, 128)
        return carry

    lax.fori_loop(0, OWNERS // 8, unpack_out, 0)

    def norm_rows(k, carry):
        at = pl.multiple_of(k * OWNERS, OWNERS)
        square = jnp.zeros((OWNERS, 128), F32)
        for n in range(CHUNKS):
            part_rows = stage[pl.ds(k * CHUNKS + n, OWNERS, stride=NB_OUT), :]
            rows[pl.ds(at, OWNERS), n * 128 : (n + 1) * 128] = part_rows
            square = square + part_rows * part_rows
        mean = jnp.sum(square, axis=1, keepdims=True) * (1.0 / D)
        scaled = rows[pl.ds(at, OWNERS), :] * lax.rsqrt(mean + EPS) * norm_attn_ref[...]
        normed[pl.ds(at, OWNERS), :] = scaled.astype(BF16)
        return carry

    for k in range(MOST):
        norm_rows(k, 0)

    tags = jnp.concatenate(
        [stage[pl.ds(48 + k, OWNERS, stride=NB_OUT), :] for k in range(MOST)], axis=0
    )
    lane = iota((SLOTS, 128), 1)
    low = lane < 64
    same_tag = tags == ((lane & 63) - 1).astype(F32)
    tag_query = same_tag.astype(BF16)
    tag_key = jnp.where(same_tag | ((lane & 63) > 4), 0.0, -BIG).astype(BF16)

    def shard(step):
        which = jnp.where(step == 1, z_of[0], jnp.where(step == 2, z_of[1], z_of[2]))
        return jnp.where(step == 0, z, which)

    def at_step(step, now, *actions):
        @pl.when(step == now)
        def _():
            for action, *given in actions:
                action(*given)

    def attend(step, carry):
        which = shard(step)
        for i in range(3):
            at_step(step, i + 1, (ready, 0, i))

        def project(n, carry):
            at = pl.multiple_of(n * 256, 256)
            qkv[:, pl.ds(at, 256)] = dot(normed[...], w_in[which, :, pl.ds(at, 256)]).astype(BF16)
            return carry

        lax.fori_loop(0, 3, project, 0)

        def pair(p, carry):
            at = pl.multiple_of(p * 128, 128)
            query = qkv[:, pl.ds(at, 128)]
            key = qkv[:, pl.ds(at + 256, 128)]
            value = qkv[:, pl.ds(at + 512, 128)]
            results = []
            for h in range(2):
                mine = low if h == 0 else jnp.logical_not(low)
                keys = jnp.where(mine, key, tag_key)
                values = jnp.where(mine, value, jnp.ones_like(value))
                queries = jnp.where(mine, query, tag_query)
                blocks = []
                for b in range(3):
                    scores = lax.dot_general(
                        queries[b * 256 : (b + 1) * 256],
                        keys,
                        (((1,), (1,)), ((), ())),
                        preferred_element_type=F32,
                    )
                    highest = jnp.max(scores, axis=1, keepdims=True)
                    shifted = jnp.exp2((scores - highest) * EXP_SCALE).astype(BF16)
                    blocks.append(dot(shifted, values))
                results.append(blocks)
            for b in range(3):
                half = low[:256]
                top = jnp.where(half, results[0][b], results[1][b])
                sums = jnp.where(half, results[1][b], results[0][b])
                heads[which * 2 + p, b * 256 : (b + 1) * 256, :] = top / pltpu.roll(sums, 64, 1)
            for now in range(8):
                at_step(step * 2 + p, now, *schedule[now])
            return carry

        lax.fori_loop(0, 2, pair, 0)
        return carry

    schedule = (
        [(near, 3), (onward, 2, 0)],
        [(onward, 2, 1), (onward, 2, 2)],
        [(far, 3), (share, 2, 0), (share, 2, 1)],
        [(share, 2, 2), (onward, 3, 0)],
        [(onward, 3, 1)],
        [(onward, 3, 2), (share, 3, 0)],
        [(share, 3, 1)],
        [(share, 3, 2)],
    )
    lax.fori_loop(0, 4, attend, 0)

    for k in range(MOST):
        for n in range(CHUNKS):
            stage[pl.ds(k * CHUNKS + n, OWNERS, stride=NB_BACK), :] = heads[
                n, k * OWNERS : (k + 1) * OWNERS, :
            ]

    def pack_back(k, carry):
        at = pl.multiple_of(k * 8 * NB_BACK, 8 * NB_BACK)
        block = stage[pl.ds(at, 8 * NB_BACK), :]
        send_back[pl.ds(k * 8, 8)] = block.reshape(8, NB_BACK, 128).astype(BF16)
        return carry

    lax.fori_loop(0, OWNERS // 8, pack_back, 0)
    own_back = exchange(send_back, recv_back, sems_back)
    for i in range(3):
        ready(1, i)
    finish(send_back, recv_back, sems_back, own_back)

    def unpack_back(k, carry):
        at = pl.multiple_of(k * 8 * NB_BACK, 8 * NB_BACK)
        block = recv_back[pl.ds(k * 8, 8)].astype(F32)
        stage[pl.ds(at, 8 * NB_BACK), :] = block.reshape(8 * NB_BACK, 128)
        return carry

    lax.fori_loop(0, OWNERS // 8, unpack_back, 0)
    for k in range(MOST):
        for n in range(CHUNKS):
            normed[k * OWNERS : (k + 1) * OWNERS, n * 128 : (n + 1) * 128] = stage[
                pl.ds(k * CHUNKS + n, OWNERS, stride=NB_BACK), :
            ].astype(BF16)

    def take(n, carry):
        at = pl.multiple_of(n * 256, 256)
        qkv[0:ROWS, pl.ds(0, 256)] = dot(gather[...], normed[:, pl.ds(at, 256)]).astype(BF16)
        partial = qkv[0:ROWS, pl.ds(0, 256)]
        for m in range(4):
            to = slice(m * 256, (m + 1) * 256)
            hidden[:, to] = hidden[:, to] + dot(partial, w_out[n, :, to])
        return carry

    hidden[...] = embedded[...].astype(F32)
    lax.fori_loop(0, 4, take, 0)
    values = hidden[...]
    mean = jnp.sum(values * values, axis=1, keepdims=True) * (1.0 / D)
    normed[0:ROWS, :] = (values * lax.rsqrt(mean + EPS) * norm_mlp_ref[...]).astype(BF16)
    total[...] = hidden[...]

    def mlp(step, carry):
        which = shard(step)
        for i in range(3):
            at_step(step, i + 1, (ready, 2, i), (ready, 3, i))

        def widen(n, carry):
            at = pl.multiple_of(n * 256, 256)
            up = dot(normed[0:ROWS, :], w_up[which, :, pl.ds(at, 256)])
            normed[ROWS:SLOTS, pl.ds(at, 256)] = jax.nn.gelu(up).astype(BF16)
            return carry

        lax.fori_loop(0, 4, widen, 0)

        def narrow(n, carry):
            at = pl.multiple_of(n * 256, 256)
            total[:, pl.ds(at, 256)] = total[:, pl.ds(at, 256)] + dot(
                normed[ROWS:SLOTS, :], w_down[which, :, pl.ds(at, 256)]
            )
            return carry

        lax.fori_loop(0, 4, narrow, 0)
        return carry

    lax.fori_loop(0, 4, mlp, 0)
    out_ref[...] = total[...].astype(BF16)
    for w in range(4):
        for slot in range(PER_WEIGHT):
            copy_of(w, slot).wait_send()


def local(
    patches, fields, route, frame, embed, norm_attn, attn_in, attn_out, norm_mlp, mlp_in, mlp_out
):
    by_field = jnp.transpose(patches, (1, 0, 2))
    whole = pl.BlockSpec(memory_space=pl.ANY)
    vmem = pl.BlockSpec(memory_space=pltpu.VMEM)
    return pl.pallas_call(
        kernel,
        out_shape=jax.ShapeDtypeStruct((ROWS, D), BF16),
        in_specs=[whole, whole, vmem, vmem, vmem, vmem, vmem, whole, whole, whole, whole],
        out_specs=vmem,
        scratch_shapes=[
            pltpu.VMEM((4, D, 768), BF16),
            pltpu.VMEM((4, 256, D), BF16),
            pltpu.VMEM((4, D, D), BF16),
            pltpu.VMEM((4, D, D), BF16),
            pltpu.VMEM((D, 768), BF16),
            pltpu.VMEM((FIELDS, PATCH, D), BF16),
            pltpu.VMEM((FIELDS, ROWS, PATCH), BF16),
            pltpu.VMEM((ROWS, D), BF16),
            pltpu.VMEM((OWNERS * NB_OUT, 128), F32),
            pltpu.VMEM((OWNERS, NB_OUT, 128), BF16),
            pltpu.VMEM((OWNERS, NB_OUT, 128), BF16),
            pltpu.VMEM((OWNERS, NB_BACK, 128), BF16),
            pltpu.VMEM((OWNERS, NB_BACK, 128), BF16),
            pltpu.VMEM((SLOTS, D), F32),
            pltpu.VMEM((SLOTS, D), BF16),
            pltpu.VMEM((SLOTS, 768), BF16),
            pltpu.VMEM((CHUNKS, SLOTS, 128), F32),
            pltpu.VMEM((ROWS, D), F32),
            pltpu.VMEM((ROWS, D), F32),
            pltpu.VMEM((ROWS, SLOTS), BF16),
            pltpu.SemaphoreType.DMA((6,)),
            pltpu.SemaphoreType.DMA((6,)),
            pltpu.SemaphoreType.DMA((4 * PER_WEIGHT,)),
            pltpu.SemaphoreType.DMA((4 * PER_WEIGHT,)),
            pltpu.SemaphoreType.REGULAR((3,)),
        ],
        compiler_params=pltpu.CompilerParams(
            collective_id=0, has_side_effects=True, vmem_limit_bytes=62 * 1024 * 1024
        ),
        cost_estimate=pl.CostEstimate(
            flops=25_000_000_000, bytes_accessed=16_000_000, transcendentals=11_000_000
        ),
    )(
        by_field,
        embed,
        route,
        frame,
        fields,
        norm_attn.reshape(1, D),
        norm_mlp.reshape(1, D),
        attn_in,
        attn_out,
        mlp_in,
        mlp_out,
    )


def solution(mesh):
    return jax.shard_map(
        local,
        mesh=mesh,
        in_specs=(
            P(("loader", "pack"), None, None),
            P(("loader", "pack")),
            P(("loader", "pack")),
            P(("loader", "pack")),
            P(),
            P(),
            P(None, "pack"),
            P("pack", None),
            P(),
            P(None, "pack"),
            P("pack", None),
        ),
        out_specs=P(("loader", "pack"), None),
        check_vma=False,
    )
```

```python
import functools

import jax
import jax.numpy as jnp
from jax import lax
from jax.experimental import pallas as pl
from jax.experimental.pallas import tpu as pltpu
from jax.sharding import PartitionSpec as P

D = 1024
FIELDS = 11
PATCH = 256
ROWS = 384
OWNERS = 128
MOST = 6
SLOTS = 768
CHUNKS = D // 128
NB_OUT = 56
NB_BACK = 48
EPS = 1e-06
BIG = 1e30
EXP_SCALE = 1.4426950408889634 / 8.0
MESH = pl.DeviceIdType.MESH
F32 = jnp.float32
BF16 = jnp.bfloat16

PER_WEIGHT = 23
WIDE = (3,)


def device(x, y, c, z):
    return (((x % 4) * 4 + y % 4) * 2 + c % 2, z % 4)


def dot(a, b):
    return jnp.dot(a, b, preferred_element_type=F32)


def iota(shape, dim):
    return lax.broadcasted_iota(jnp.int32, shape, dim)


def kernel(
    patches_ref,
    embed_ref,
    route_ref,
    frame_ref,
    fields_ref,
    norm_attn_ref,
    norm_mlp_ref,
    attn_in_ref,
    attn_out_ref,
    mlp_in_ref,
    mlp_out_ref,
    out_ref,
    w_in,
    w_out,
    w_up,
    w_down,
    raw_in,
    embed_v,
    flat,
    embedded,
    stage,
    send_out,
    recv_out,
    send_back,
    recv_back,
    rows,
    normed,
    qkv,
    heads,
    hidden,
    total,
    gather,
    local_sem,
    row_sem,
    wsend,
    wrecv,
    here,
):
    loader = lax.axis_index("loader")
    z = lax.axis_index("pack")
    x, y, c = loader // 8, (loader // 2) % 4, loader % 2
    me = loader * 4 + z
    r = jnp.where(c == 0, x, y)

    loads = []

    def load(src, dst):
        copy = pltpu.make_async_copy(src, dst, local_sem.at[len(loads)])
        copy.start()
        loads.append(copy)
        return copy

    get_in = load(attn_in_ref, raw_in)
    get_embed = load(embed_ref, embed_v)
    get_patches = load(patches_ref, flat)
    get_out = load(attn_out_ref, w_out.at[z])
    get_up = load(mlp_in_ref, w_up.at[z])
    get_down = load(mlp_out_ref, w_down.at[z])

    def peer(k):
        dx, dc = k % 4, (k // 64 + k) % 2
        dy, dz = (k // 4 + dx) % 4, (k // 16 + 4 - dx) % 4
        px, py, pc, pz = (x + dx) % 4, (y + dy) % 4, (c + dc) % 2, (z + dz) % 4
        to = (px * 4 + py) * 2 + pc
        return (to, pz), to * 4 + pz

    barrier = pltpu.get_barrier_semaphore()
    line_x = [device(x + k, y, c, z) for k in (1, 3, 2)]
    line_y = [device(x, y + k, c, z) for k in (1, 3, 2)]
    line_z = [device(x, y, c, z + k) for k in (1, 3, 2)]
    for to in line_x + line_y + line_z + [device(x, y, c + 1, z)]:
        pl.semaphore_signal(barrier, inc=1, device_id=to, device_id_type=MESH)

    def greet(line, stage):
        for to in line:
            pl.semaphore_signal(here.at[stage], inc=1, device_id=to, device_id_type=MESH)

    def heard(stage):
        pl.semaphore_wait(here.at[stage], 3)

    get_in.wait()

    def reorder(n, carry):
        col = iota((768, 256), 1)
        source = (col >> 6) * 192 + n * 64 + (col & 63)
        pick = (iota((768, 256), 0) == source).astype(BF16)
        at = pl.multiple_of(n * 256, 256)
        w_in[z, :, pl.ds(at, 256)] = dot(raw_in[...], pick).astype(BF16)
        return carry

    lax.fori_loop(0, 3, reorder, 0)

    weights = (w_in, w_out, w_up, w_down)
    z_of = ((z + 3) % 4, (z + 1) % 4, (z + 2) % 4)
    up_z, down_z = device(x, y, c, z + 1), device(x, y, c, z + 3)
    one = jnp.where(c == 0, 1, 0)
    up_r = device(x + one, y + 1 - one, c, z)
    down_r = device(x + 3 * one, y + 3 - 3 * one, c, z)
    other = device(x, y, c + 1, z)

    def part(w, which, q, half=None):
        size = weights[w].shape[1] // 8
        start = (c * 4 + q % 4) * size
        if half is not None:
            size = size // 2
            start = start + half * size
        return weights[w].at[which, pl.ds(pl.multiple_of(start, size), size)]

    def copy_of(w, slot):
        if slot < 2:
            block, to = part(w, z, r), (up_z, down_z)[slot]
        elif slot < 4:
            block, to = part(w, z_of[slot - 2], r, slot - 2), (up_z, down_z)[slot - 2]
        elif slot < 16:
            i, step = (slot - 4) // 4, (slot - 4) % 4
            to = (up_r, down_r)[step % 2]
            if step < 2:
                block = part(w, z_of[i], r)
            else:
                block = part(w, z_of[i], r + (3 if step == 2 else 1), step - 2)
        elif slot < 19:
            size = weights[w].shape[1] // 2
            at = pl.multiple_of(c * size, size)
            block, to = weights[w].at[z_of[slot - 16], pl.ds(at, size)], other
        elif slot < 21:
            block, to = part(w, z, r + 2), (up_z, down_z)[slot - 19]
        else:
            block, to = part(w, z_of[slot - 21], r + 2, slot - 21), (up_z, down_z)[slot - 21]
        return pltpu.make_async_remote_copy(
            block,
            block,
            wsend.at[w * PER_WEIGHT + slot],
            wrecv.at[w * PER_WEIGHT + slot],
            device_id=to,
            device_id_type=MESH,
        )

    def send(w, slot):
        copy_of(w, slot).start()

    def arrived(w, slot):
        copy_of(w, slot).wait_recv()

    def slots_of(w):
        if w in WIDE:
            return [k for k in range(PER_WEIGHT) if k < 4 or k >= 16 or k % 4 < 2]
        return range(19)

    def begin(w):
        send(w, 0)
        send(w, 1)
        if w in WIDE:
            send(w, 19)
            send(w, 20)

    def ring(w, i):
        send(w, 4 + 4 * i)
        send(w, 5 + 4 * i)

    def near(w):
        arrived(w, 0)
        send(w, 2)
        ring(w, 0)
        arrived(w, 1)
        send(w, 3)
        ring(w, 1)
        if w in WIDE:
            arrived(w, 19)
            send(w, 21)
            arrived(w, 20)
            send(w, 22)

    def far(w):
        arrived(w, 2)
        arrived(w, 3)
        ring(w, 2)
        if w in WIDE:
            arrived(w, 21)
            arrived(w, 22)

    def onward(w, i):
        if w in WIDE:
            return
        arrived(w, 4 + 4 * i)
        send(w, 6 + 4 * i)
        arrived(w, 5 + 4 * i)
        send(w, 7 + 4 * i)

    def share(w, i):
        last = 4 if w in WIDE else 6
        arrived(w, last + 4 * i)
        arrived(w, last + 1 + 4 * i)
        send(w, 16 + i)

    def ready(w, i):
        arrived(w, 16 + i)

    pl.semaphore_wait(barrier, 10)
    begin(0)
    greet(line_z, 0)
    get_out.wait()

    route_row = route_ref[...].reshape(1, ROWS)
    frame_row = frame_ref[...].reshape(1, ROWS).astype(F32)
    eye = iota((ROWS, ROWS), 0) == iota((ROWS, ROWS), 1)

    def column(row):
        return jnp.sum(jnp.where(eye, row, 0.0), axis=1, keepdims=True)

    onehot = (iota((OWNERS, ROWS), 0) == route_row).astype(F32)
    before = (iota((ROWS, ROWS), 0) < iota((ROWS, ROWS), 1)).astype(BF16)
    rank_row = jnp.sum(dot(onehot.astype(BF16), before) * onehot, axis=0, keepdims=True)
    heard(0)
    fields_col = column(fields_ref[...].reshape(1, ROWS).astype(F32))
    greet(line_y, 1)

    get_embed.wait()
    get_patches.wait()
    for f in range(FIELDS):
        pixels = flat[f]
        flat[f] = jnp.where(fields_col > float(f), pixels.astype(F32), 0.0).astype(BF16)

    def embed_tile(n, carry):
        at = pl.multiple_of(n * 1024, 1024)
        acc = dot(flat[0], embed_v[0, :, pl.ds(at, 1024)])
        for f in range(1, FIELDS):
            acc = acc + dot(flat[f], embed_v[f, :, pl.ds(at, 1024)])
        embedded[:, pl.ds(at, 1024)] = acc.astype(BF16)
        return carry

    lax.fori_loop(0, 1, embed_tile, 0)

    heard(1)
    greet(line_x, 2)
    near(0)

    for k in range(MOST):
        place = onehot * (rank_row == float(k)).astype(F32)
        tag = jnp.sum(place * (frame_row + 1.0), axis=1, keepdims=True) - 1.0
        placed = dot(place.astype(BF16), embedded[...])
        for n in range(CHUNKS):
            stage[pl.ds(k * CHUNKS + n, OWNERS, stride=NB_OUT), :] = placed[
                :, n * 128 : (n + 1) * 128
            ]
        stage[pl.ds(48 + k, OWNERS, stride=NB_OUT), :] = jnp.broadcast_to(tag, (OWNERS, 128))
    for k in range(48 + MOST, NB_OUT):
        stage[pl.ds(k, OWNERS, stride=NB_OUT), :] = jnp.zeros((OWNERS, 128), F32)

    def pack_out(k, carry):
        at = pl.multiple_of(k * 8 * NB_OUT, 8 * NB_OUT)
        block = stage[pl.ds(at, 8 * NB_OUT), :]
        send_out[pl.ds(k * 8, 8)] = block.reshape(8, NB_OUT, 128).astype(BF16)
        return carry

    lax.fori_loop(0, OWNERS // 8, pack_out, 0)

    heard(2)

    def exchange(source, target, sems):
        own = pltpu.make_async_copy(source.at[me], target.at[me], sems[2])
        own.start()

        def one_peer(k, carry):
            to, index = peer(k)
            pltpu.make_async_remote_copy(
                source.at[index],
                target.at[me],
                sems[0],
                sems[1],
                device_id=to,
                device_id_type=MESH,
            ).start()
            return carry

        lax.fori_loop(1, OWNERS, one_peer, 0)
        return own

    def finish(source, target, sems, own):
        own.wait()
        pltpu.make_async_remote_copy(
            source.at[pl.ds(0, OWNERS - 1)],
            target.at[pl.ds(0, OWNERS - 1)],
            sems[0],
            sems[1],
            device_id=other,
            device_id_type=MESH,
        ).wait()

    sems_out = (row_sem.at[0], row_sem.at[1], row_sem.at[2])
    sems_back = (row_sem.at[3], row_sem.at[4], row_sem.at[5])

    own_out = exchange(send_out, recv_out, sems_out)
    route_col = column(route_row.astype(F32))
    rank_col = column(rank_row)
    owner_lane = iota((ROWS, OWNERS), 1).astype(F32)
    for k in range(MOST):
        gather[:, k * OWNERS : (k + 1) * OWNERS] = (
            (owner_lane == route_col) & (rank_col == float(k))
        ).astype(BF16)
    begin(1)
    get_up.wait()
    get_down.wait()
    begin(2)
    far(0)
    onward(0, 0)
    onward(0, 1)
    onward(0, 2)
    share(0, 0)
    share(0, 1)
    share(0, 2)
    finish(send_out, recv_out, sems_out, own_out)

    def unpack_out(k, carry):
        at = pl.multiple_of(k * 8 * NB_OUT, 8 * NB_OUT)
        block = recv_out[pl.ds(k * 8, 8)].astype(F32)
        stage[pl.ds(at, 8 * NB_OUT), :] = block.reshape(8 * NB_OUT, 128)
        return carry

    lax.fori_loop(0, OWNERS // 8, unpack_out, 0)

    def norm_rows(k, carry):
        at = pl.multiple_of(k * OWNERS, OWNERS)
        square = jnp.zeros((OWNERS, 128), F32)
        for n in range(CHUNKS):
            part_rows = stage[pl.ds(k * CHUNKS + n, OWNERS, stride=NB_OUT), :]
            rows[pl.ds(at, OWNERS), n * 128 : (n + 1) * 128] = part_rows
            square = square + part_rows * part_rows
        mean = jnp.sum(square, axis=1, keepdims=True) * (1.0 / D)
        scaled = rows[pl.ds(at, OWNERS), :] * lax.rsqrt(mean + EPS) * norm_attn_ref[...]
        normed[pl.ds(at, OWNERS), :] = scaled.astype(BF16)
        return carry

    for k in range(MOST):
        norm_rows(k, 0)

    tags = jnp.concatenate(
        [stage[pl.ds(48 + k, OWNERS, stride=NB_OUT), :] for k in range(MOST)], axis=0
    )
    lane = iota((SLOTS, 128), 1)
    low = lane < 64
    same_tag = tags == ((lane & 63) - 1).astype(F32)
    tag_query = same_tag.astype(BF16)
    tag_key = jnp.where(same_tag | ((lane & 63) > 4), 0.0, -BIG).astype(BF16)

    def shard(step):
        which = jnp.where(step == 1, z_of[0], jnp.where(step == 2, z_of[1], z_of[2]))
        return jnp.where(step == 0, z, which)

    def at_step(step, now, *actions):
        @pl.when(step == now)
        def _():
            for action, *given in actions:
                action(*given)

    def attend(step, carry):
        which = shard(step)
        for i in range(3):
            at_step(step, i + 1, (ready, 0, i))

        def project(n, carry):
            at = pl.multiple_of(n * 768, 768)
            qkv[:, pl.ds(at, 768)] = dot(normed[...], w_in[which, :, pl.ds(at, 768)]).astype(BF16)
            return carry

        lax.fori_loop(0, 1, project, 0)

        def pair(p, carry):
            at = pl.multiple_of(p * 128, 128)
            query = qkv[:, pl.ds(at, 128)]
            key = qkv[:, pl.ds(at + 256, 128)]
            value = qkv[:, pl.ds(at + 512, 128)]
            results = []
            for h in range(2):
                mine = low if h == 0 else jnp.logical_not(low)
                keys = jnp.where(mine, key, tag_key)
                values = jnp.where(mine, value, jnp.ones_like(value))
                queries = jnp.where(mine, query, tag_query)
                blocks = []
                for b in range(2):
                    scores = lax.dot_general(
                        queries[b * 384 : (b + 1) * 384],
                        keys,
                        (((1,), (1,)), ((), ())),
                        preferred_element_type=F32,
                    )
                    highest = jnp.max(scores, axis=1, keepdims=True)
                    shifted = jnp.exp2((scores - highest) * EXP_SCALE).astype(BF16)
                    blocks.append(dot(shifted, values))
                results.append(blocks)
            for b in range(2):
                half = low[:384]
                top = jnp.where(half, results[0][b], results[1][b])
                sums = jnp.where(half, results[1][b], results[0][b])
                heads[which * 2 + p, b * 384 : (b + 1) * 384, :] = top / pltpu.roll(sums, 64, 1)
            for now in range(8):
                at_step(step * 2 + p, now, *schedule[now])
            return carry

        lax.fori_loop(0, 2, pair, 0)
        return carry

    schedule = (
        [(near, 1), (near, 2), (begin, 3)],
        [(far, 1), (far, 2)],
        [(onward, 1, 0), (onward, 1, 1), (onward, 1, 2), (onward, 2, 0)],
        [(onward, 2, 1), (near, 3)],
        [(onward, 2, 2), (share, 1, 0), (share, 1, 1), (share, 1, 2), (far, 3)],
        [(share, 2, 0), (share, 2, 1), (share, 2, 2)],
        [(share, 3, 0), (share, 3, 1)],
        [(share, 3, 2)],
    )
    lax.fori_loop(0, 4, attend, 0)

    for k in range(MOST):
        for n in range(CHUNKS):
            stage[pl.ds(k * CHUNKS + n, OWNERS, stride=NB_BACK), :] = heads[
                n, k * OWNERS : (k + 1) * OWNERS, :
            ]

    def pack_back(k, carry):
        at = pl.multiple_of(k * 8 * NB_BACK, 8 * NB_BACK)
        block = stage[pl.ds(at, 8 * NB_BACK), :]
        send_back[pl.ds(k * 8, 8)] = block.reshape(8, NB_BACK, 128).astype(BF16)
        return carry

    lax.fori_loop(0, OWNERS // 8, pack_back, 0)
    own_back = exchange(send_back, recv_back, sems_back)
    for i in range(3):
        ready(1, i)
    finish(send_back, recv_back, sems_back, own_back)

    def unpack_back(k, carry):
        at = pl.multiple_of(k * 8 * NB_BACK, 8 * NB_BACK)
        block = recv_back[pl.ds(k * 8, 8)].astype(F32)
        stage[pl.ds(at, 8 * NB_BACK), :] = block.reshape(8 * NB_BACK, 128)
        return carry

    lax.fori_loop(0, OWNERS // 8, unpack_back, 0)
    for k in range(MOST):
        for n in range(CHUNKS):
            normed[k * OWNERS : (k + 1) * OWNERS, n * 128 : (n + 1) * 128] = stage[
                pl.ds(k * CHUNKS + n, OWNERS, stride=NB_BACK), :
            ].astype(BF16)

    def take(n, carry):
        at = pl.multiple_of(n * 256, 256)
        qkv[0:ROWS, pl.ds(0, 256)] = dot(gather[...], normed[:, pl.ds(at, 256)]).astype(BF16)
        partial = qkv[0:ROWS, pl.ds(0, 256)]
        for m in range(4):
            to = slice(m * 256, (m + 1) * 256)
            hidden[:, to] = hidden[:, to] + dot(partial, w_out[n, :, to])
        return carry

    hidden[...] = embedded[...].astype(F32)
    lax.fori_loop(0, 4, take, 0)
    values = hidden[...]
    mean = jnp.sum(values * values, axis=1, keepdims=True) * (1.0 / D)
    normed[0:ROWS, :] = (values * lax.rsqrt(mean + EPS) * norm_mlp_ref[...]).astype(BF16)
    total[...] = hidden[...]

    def mlp(step, carry):
        which = shard(step)
        for i in range(3):
            at_step(step, i + 1, (ready, 2, i), (ready, 3, i))

        def widen(n, carry):
            at = pl.multiple_of(n * 1024, 1024)
            up = dot(normed[0:ROWS, :], w_up[which, :, pl.ds(at, 1024)])
            normed[ROWS:SLOTS, pl.ds(at, 1024)] = jax.nn.gelu(up).astype(BF16)
            return carry

        lax.fori_loop(0, 1, widen, 0)

        def narrow(n, carry):
            at = pl.multiple_of(n * 1024, 1024)
            total[:, pl.ds(at, 1024)] = total[:, pl.ds(at, 1024)] + dot(
                normed[ROWS:SLOTS, :], w_down[which, :, pl.ds(at, 1024)]
            )
            return carry

        lax.fori_loop(0, 1, narrow, 0)
        return carry

    lax.fori_loop(0, 4, mlp, 0)
    out_ref[...] = total[...].astype(BF16)
    for w in range(4):
        for slot in slots_of(w):
            copy_of(w, slot).wait_send()


def local(
    patches, fields, route, frame, embed, norm_attn, attn_in, attn_out, norm_mlp, mlp_in, mlp_out
):
    by_field = jnp.transpose(patches, (1, 0, 2))
    whole = pl.BlockSpec(memory_space=pl.ANY)
    vmem = pl.BlockSpec(memory_space=pltpu.VMEM)
    return pl.pallas_call(
        kernel,
        out_shape=jax.ShapeDtypeStruct((ROWS, D), BF16),
        in_specs=[whole, whole, vmem, vmem, vmem, vmem, vmem, whole, whole, whole, whole],
        out_specs=vmem,
        scratch_shapes=[
            pltpu.VMEM((4, D, 768), BF16),
            pltpu.VMEM((4, 256, D), BF16),
            pltpu.VMEM((4, D, D), BF16),
            pltpu.VMEM((4, D, D), BF16),
            pltpu.VMEM((D, 768), BF16),
            pltpu.VMEM((FIELDS, PATCH, D), BF16),
            pltpu.VMEM((FIELDS, ROWS, PATCH), BF16),
            pltpu.VMEM((ROWS, D), BF16),
            pltpu.VMEM((OWNERS * NB_OUT, 128), F32),
            pltpu.VMEM((OWNERS, NB_OUT, 128), BF16),
            pltpu.VMEM((OWNERS, NB_OUT, 128), BF16),
            pltpu.VMEM((OWNERS, NB_BACK, 128), BF16),
            pltpu.VMEM((OWNERS, NB_BACK, 128), BF16),
            pltpu.VMEM((SLOTS, D), F32),
            pltpu.VMEM((SLOTS, D), BF16),
            pltpu.VMEM((SLOTS, 768), BF16),
            pltpu.VMEM((CHUNKS, SLOTS, 128), F32),
            pltpu.VMEM((ROWS, D), F32),
            pltpu.VMEM((ROWS, D), F32),
            pltpu.VMEM((ROWS, SLOTS), BF16),
            pltpu.SemaphoreType.DMA((6,)),
            pltpu.SemaphoreType.DMA((6,)),
            pltpu.SemaphoreType.DMA((4 * PER_WEIGHT,)),
            pltpu.SemaphoreType.DMA((4 * PER_WEIGHT,)),
            pltpu.SemaphoreType.REGULAR((3,)),
        ],
        compiler_params=pltpu.CompilerParams(
            collective_id=0, has_side_effects=True, vmem_limit_bytes=62 * 1024 * 1024
        ),
        cost_estimate=pl.CostEstimate(
            flops=25_000_000_000, bytes_accessed=16_000_000, transcendentals=11_000_000
        ),
    )(
        by_field,
        embed,
        route,
        frame,
        fields,
        norm_attn.reshape(1, D),
        norm_mlp.reshape(1, D),
        attn_in,
        attn_out,
        mlp_in,
        mlp_out,
    )


def solution(mesh):
    return jax.shard_map(
        local,
        mesh=mesh,
        in_specs=(
            P(("loader", "pack"), None, None),
            P(("loader", "pack")),
            P(("loader", "pack")),
            P(("loader", "pack")),
            P(),
            P(),
            P(None, "pack"),
            P("pack", None),
            P(),
            P(None, "pack"),
            P("pack", None),
        ),
        out_specs=P(("loader", "pack"), None),
        check_vma=False,
    )
```

```python
import functools

import jax
import jax.numpy as jnp
from jax import lax
from jax.experimental import pallas as pl
from jax.experimental.pallas import tpu as pltpu
from jax.sharding import PartitionSpec as P

D = 1024
FIELDS = 11
PATCH = 256
ROWS = 384
OWNERS = 128
MOST = 6
SLOTS = 768
CHUNKS = D // 128
NB_OUT = 56
NB_BACK = 48
EPS = 1e-06
BIG = 1e30
EXP_SCALE = 1.4426950408889634 / 8.0
MESH = pl.DeviceIdType.MESH
F32 = jnp.float32
BF16 = jnp.bfloat16

PER_WEIGHT = 23
WIDE = (3,)


def device(x, y, c, z):
    return (((x % 4) * 4 + y % 4) * 2 + c % 2, z % 4)


def dot(a, b):
    return jnp.dot(a, b, preferred_element_type=F32)


def iota(shape, dim):
    return lax.broadcasted_iota(jnp.int32, shape, dim)


def kernel(
    patches_ref,
    embed_ref,
    route_ref,
    frame_ref,
    fields_ref,
    norm_attn_ref,
    norm_mlp_ref,
    attn_in_ref,
    attn_out_ref,
    mlp_in_ref,
    mlp_out_ref,
    out_ref,
    w_in,
    w_out,
    w_up,
    w_down,
    raw_in,
    embed_v,
    flat,
    embedded,
    stage,
    send_out,
    recv_out,
    send_back,
    recv_back,
    rows,
    normed,
    qkv,
    hidden,
    total,
    gather,
    local_sem,
    row_sem,
    wsend,
    wrecv,
    here,
):
    loader = lax.axis_index("loader")
    z = lax.axis_index("pack")
    x, y, c = loader // 8, (loader // 2) % 4, loader % 2
    me = loader * 4 + z
    r = jnp.where(c == 0, x, y)

    loads = []

    def load(src, dst):
        copy = pltpu.make_async_copy(src, dst, local_sem.at[len(loads)])
        copy.start()
        loads.append(copy)
        return copy

    get_in = load(attn_in_ref, raw_in)
    get_embed = load(embed_ref, embed_v)
    get_patches = load(patches_ref, flat)
    get_out = load(attn_out_ref, w_out.at[z])
    get_up = load(mlp_in_ref, w_up.at[z])
    get_down = load(mlp_out_ref, w_down.at[z])

    def peer(k):
        dx, dc = k % 4, (k // 64 + k) % 2
        dy, dz = (k // 4 + dx) % 4, (k // 16 + 4 - dx) % 4
        px, py, pc, pz = (x + dx) % 4, (y + dy) % 4, (c + dc) % 2, (z + dz) % 4
        to = (px * 4 + py) * 2 + pc
        return (to, pz), to * 4 + pz

    barrier = pltpu.get_barrier_semaphore()
    line_x = [device(x + k, y, c, z) for k in (1, 3, 2)]
    line_y = [device(x, y + k, c, z) for k in (1, 3, 2)]
    line_z = [device(x, y, c, z + k) for k in (1, 3, 2)]
    for to in line_x + line_y + line_z + [device(x, y, c + 1, z)]:
        pl.semaphore_signal(barrier, inc=1, device_id=to, device_id_type=MESH)

    def greet(line, stage):
        for to in line:
            pl.semaphore_signal(here.at[stage], inc=1, device_id=to, device_id_type=MESH)

    def heard(stage):
        pl.semaphore_wait(here.at[stage], 3)

    get_in.wait()

    def reorder(n, carry):
        col = iota((768, 256), 1)
        source = (col >> 6) * 192 + n * 64 + (col & 63)
        pick = (iota((768, 256), 0) == source).astype(BF16)
        at = pl.multiple_of(n * 256, 256)
        w_in[z, :, pl.ds(at, 256)] = dot(raw_in[...], pick).astype(BF16)
        return carry

    lax.fori_loop(0, 3, reorder, 0)

    weights = (w_in, w_out, w_up, w_down)
    z_of = ((z + 3) % 4, (z + 1) % 4, (z + 2) % 4)
    up_z, down_z = device(x, y, c, z + 1), device(x, y, c, z + 3)
    one = jnp.where(c == 0, 1, 0)
    up_r = device(x + one, y + 1 - one, c, z)
    down_r = device(x + 3 * one, y + 3 - 3 * one, c, z)
    other = device(x, y, c + 1, z)

    def part(w, which, q, half=None):
        size = weights[w].shape[1] // 8
        start = (c * 4 + q % 4) * size
        if half is not None:
            size = size // 2
            start = start + half * size
        return weights[w].at[which, pl.ds(pl.multiple_of(start, size), size)]

    def copy_of(w, slot):
        if slot < 2:
            block, to = part(w, z, r), (up_z, down_z)[slot]
        elif slot < 4:
            block, to = part(w, z_of[slot - 2], r, slot - 2), (up_z, down_z)[slot - 2]
        elif slot < 16:
            i, step = (slot - 4) // 4, (slot - 4) % 4
            to = (up_r, down_r)[step % 2]
            if step < 2:
                block = part(w, z_of[i], r)
            else:
                block = part(w, z_of[i], r + (3 if step == 2 else 1), step - 2)
        elif slot < 19:
            size = weights[w].shape[1] // 2
            at = pl.multiple_of(c * size, size)
            block, to = weights[w].at[z_of[slot - 16], pl.ds(at, size)], other
        elif slot < 21:
            block, to = part(w, z, r + 2), (up_z, down_z)[slot - 19]
        else:
            block, to = part(w, z_of[slot - 21], r + 2, slot - 21), (up_z, down_z)[slot - 21]
        return pltpu.make_async_remote_copy(
            block,
            block,
            wsend.at[w * PER_WEIGHT + slot],
            wrecv.at[w * PER_WEIGHT + slot],
            device_id=to,
            device_id_type=MESH,
        )

    def send(w, slot):
        copy_of(w, slot).start()

    def arrived(w, slot):
        copy_of(w, slot).wait_recv()

    def slots_of(w):
        if w in WIDE:
            return [k for k in range(PER_WEIGHT) if k < 4 or k >= 16 or k % 4 < 2]
        return range(19)

    def begin(w):
        send(w, 0)
        send(w, 1)
        if w in WIDE:
            send(w, 19)
            send(w, 20)

    def ring(w, i):
        send(w, 4 + 4 * i)
        send(w, 5 + 4 * i)

    def near(w):
        arrived(w, 0)
        send(w, 2)
        ring(w, 0)
        arrived(w, 1)
        send(w, 3)
        ring(w, 1)
        if w in WIDE:
            arrived(w, 19)
            send(w, 21)
            arrived(w, 20)
            send(w, 22)

    def far(w):
        arrived(w, 2)
        arrived(w, 3)
        ring(w, 2)
        if w in WIDE:
            arrived(w, 21)
            arrived(w, 22)

    def onward(w, i):
        if w in WIDE:
            return
        arrived(w, 4 + 4 * i)
        send(w, 6 + 4 * i)
        arrived(w, 5 + 4 * i)
        send(w, 7 + 4 * i)

    def share(w, i):
        last = 4 if w in WIDE else 6
        arrived(w, last + 4 * i)
        arrived(w, last + 1 + 4 * i)
        send(w, 16 + i)

    def ready(w, i):
        arrived(w, 16 + i)

    pl.semaphore_wait(barrier, 10)
    begin(0)
    greet(line_z, 0)
    get_out.wait()

    route_row = route_ref[...].reshape(1, ROWS)
    frame_row = frame_ref[...].reshape(1, ROWS).astype(F32)
    eye = iota((ROWS, ROWS), 0) == iota((ROWS, ROWS), 1)

    def column(row):
        return jnp.sum(jnp.where(eye, row, 0.0), axis=1, keepdims=True)

    onehot = (iota((OWNERS, ROWS), 0) == route_row).astype(F32)
    before = (iota((ROWS, ROWS), 0) < iota((ROWS, ROWS), 1)).astype(BF16)
    rank_row = jnp.sum(dot(onehot.astype(BF16), before) * onehot, axis=0, keepdims=True)
    heard(0)
    fields_col = column(fields_ref[...].reshape(1, ROWS).astype(F32))
    greet(line_y, 1)

    get_embed.wait()
    get_patches.wait()
    for f in range(FIELDS):
        pixels = flat[f]
        flat[f] = jnp.where(fields_col > float(f), pixels.astype(F32), 0.0).astype(BF16)

    def embed_tile(n, carry):
        at = pl.multiple_of(n * 1024, 1024)
        acc = dot(flat[0], embed_v[0, :, pl.ds(at, 1024)])
        for f in range(1, FIELDS):
            acc = acc + dot(flat[f], embed_v[f, :, pl.ds(at, 1024)])
        embedded[:, pl.ds(at, 1024)] = acc.astype(BF16)
        return carry

    lax.fori_loop(0, 1, embed_tile, 0)

    heard(1)
    greet(line_x, 2)
    near(0)

    for k in range(MOST):
        place = onehot * (rank_row == float(k)).astype(F32)
        tag = jnp.sum(place * (frame_row + 1.0), axis=1, keepdims=True) - 1.0
        placed = dot(place.astype(BF16), embedded[...])
        for n in range(CHUNKS):
            stage[pl.ds(k * CHUNKS + n, OWNERS, stride=NB_OUT), :] = placed[
                :, n * 128 : (n + 1) * 128
            ]
        stage[pl.ds(48 + k, OWNERS, stride=NB_OUT), :] = jnp.broadcast_to(tag, (OWNERS, 128))
    for k in range(48 + MOST, NB_OUT):
        stage[pl.ds(k, OWNERS, stride=NB_OUT), :] = jnp.zeros((OWNERS, 128), F32)

    def pack_out(k, carry):
        at = pl.multiple_of(k * 8 * NB_OUT, 8 * NB_OUT)
        block = stage[pl.ds(at, 8 * NB_OUT), :]
        send_out[pl.ds(k * 8, 8)] = block.reshape(8, NB_OUT, 128).astype(BF16)
        return carry

    lax.fori_loop(0, OWNERS // 8, pack_out, 0)

    heard(2)

    def exchange(source, target, sems):
        own = pltpu.make_async_copy(source.at[me], target.at[me], sems[2])
        own.start()

        def one_peer(k, carry):
            to, index = peer(k)
            pltpu.make_async_remote_copy(
                source.at[index],
                target.at[me],
                sems[0],
                sems[1],
                device_id=to,
                device_id_type=MESH,
            ).start()
            return carry

        lax.fori_loop(1, OWNERS, one_peer, 0)
        return own

    def finish(source, target, sems, own):
        own.wait()
        pltpu.make_async_remote_copy(
            source.at[pl.ds(0, OWNERS - 1)],
            target.at[pl.ds(0, OWNERS - 1)],
            sems[0],
            sems[1],
            device_id=other,
            device_id_type=MESH,
        ).wait()

    sems_out = (row_sem.at[0], row_sem.at[1], row_sem.at[2])
    sems_back = (row_sem.at[3], row_sem.at[4], row_sem.at[5])

    own_out = exchange(send_out, recv_out, sems_out)
    route_col = column(route_row.astype(F32))
    rank_col = column(rank_row)
    owner_lane = iota((ROWS, OWNERS), 1).astype(F32)
    for k in range(MOST):
        gather[:, k * OWNERS : (k + 1) * OWNERS] = (
            (owner_lane == route_col) & (rank_col == float(k))
        ).astype(BF16)
    begin(1)
    get_up.wait()
    get_down.wait()
    begin(2)
    far(0)
    onward(0, 0)
    onward(0, 1)
    onward(0, 2)
    share(0, 0)
    share(0, 1)
    share(0, 2)
    finish(send_out, recv_out, sems_out, own_out)

    def unpack_out(k, carry):
        at = pl.multiple_of(k * 8 * NB_OUT, 8 * NB_OUT)
        block = recv_out[pl.ds(k * 8, 8)].astype(F32)
        stage[pl.ds(at, 8 * NB_OUT), :] = block.reshape(8 * NB_OUT, 128)
        return carry

    lax.fori_loop(0, OWNERS // 8, unpack_out, 0)

    def norm_rows(k, carry):
        at = pl.multiple_of(k * OWNERS, OWNERS)
        square = jnp.zeros((OWNERS, 128), F32)
        for n in range(CHUNKS):
            part_rows = stage[pl.ds(k * CHUNKS + n, OWNERS, stride=NB_OUT), :]
            rows[pl.ds(at, OWNERS), n * 128 : (n + 1) * 128] = part_rows
            square = square + part_rows * part_rows
        mean = jnp.sum(square, axis=1, keepdims=True) * (1.0 / D)
        scaled = rows[pl.ds(at, OWNERS), :] * lax.rsqrt(mean + EPS) * norm_attn_ref[...]
        normed[pl.ds(at, OWNERS), :] = scaled.astype(BF16)
        return carry

    for k in range(MOST):
        norm_rows(k, 0)

    tags = jnp.concatenate(
        [stage[pl.ds(48 + k, OWNERS, stride=NB_OUT), :] for k in range(MOST)], axis=0
    )
    lane = iota((SLOTS, 128), 1)
    low = lane < 64
    same_tag = tags == ((lane & 63) - 1).astype(F32)
    tag_query = same_tag.astype(BF16)
    tag_key = jnp.where(same_tag | ((lane & 63) > 4), 0.0, -BIG).astype(BF16)

    def shard(step):
        which = jnp.where(step == 1, z_of[0], jnp.where(step == 2, z_of[1], z_of[2]))
        return jnp.where(step == 0, z, which)

    def at_step(step, now, *actions):
        @pl.when(step == now)
        def _():
            for action, *given in actions:
                action(*given)

    def attend(step, carry):
        which = shard(step)
        for i in range(3):
            at_step(step, i + 1, (ready, 0, i))

        def project(n, carry):
            at = pl.multiple_of(n * 768, 768)
            qkv[:, pl.ds(at, 768)] = dot(normed[...], w_in[which, :, pl.ds(at, 768)]).astype(BF16)
            return carry

        lax.fori_loop(0, 1, project, 0)

        def pair(p, carry):
            at = pl.multiple_of(p * 128, 128)
            query = qkv[:, pl.ds(at, 128)]
            key = qkv[:, pl.ds(at + 256, 128)]
            value = qkv[:, pl.ds(at + 512, 128)]
            results = []
            for h in range(2):
                mine = low if h == 0 else jnp.logical_not(low)
                keys = jnp.where(mine, key, tag_key)
                values = jnp.where(mine, value, jnp.ones_like(value))
                queries = jnp.where(mine, query, tag_query)
                blocks = []
                for b in range(2):
                    scores = lax.dot_general(
                        queries[b * 384 : (b + 1) * 384],
                        keys,
                        (((1,), (1,)), ((), ())),
                        preferred_element_type=F32,
                    )
                    highest = jnp.max(scores, axis=1, keepdims=True)
                    shifted = jnp.exp2((scores - highest) * EXP_SCALE).astype(BF16)
                    blocks.append(dot(shifted, values))
                results.append(blocks)
            for b in range(2):
                half = low[:384]
                top = jnp.where(half, results[0][b], results[1][b])
                sums = jnp.where(half, results[1][b], results[0][b])
                result = top / pltpu.roll(sums, 64, 1)
                for k in range(3):
                    first = (b * 3 + k) * CHUNKS + which * 2 + p
                    stage[pl.ds(first, OWNERS, stride=NB_BACK), :] = result[
                        k * OWNERS : (k + 1) * OWNERS
                    ]
            for now in range(8):
                at_step(step * 2 + p, now, *schedule[now])
            return carry

        lax.fori_loop(0, 2, pair, 0)
        return carry

    schedule = (
        [(near, 1), (near, 2), (begin, 3)],
        [(far, 1), (far, 2)],
        [(onward, 1, 0), (onward, 1, 1), (onward, 1, 2), (onward, 2, 0)],
        [(onward, 2, 1), (near, 3)],
        [(onward, 2, 2), (share, 1, 0), (share, 1, 1), (share, 1, 2), (far, 3)],
        [(share, 2, 0), (share, 2, 1), (share, 2, 2)],
        [(share, 3, 0), (share, 3, 1)],
        [(share, 3, 2)],
    )
    lax.fori_loop(0, 4, attend, 0)

    def pack_back(k, carry):
        at = pl.multiple_of(k * 8 * NB_BACK, 8 * NB_BACK)
        block = stage[pl.ds(at, 8 * NB_BACK), :]
        send_back[pl.ds(k * 8, 8)] = block.reshape(8, NB_BACK, 128).astype(BF16)
        return carry

    lax.fori_loop(0, OWNERS // 8, pack_back, 0)
    own_back = exchange(send_back, recv_back, sems_back)
    for i in range(3):
        ready(1, i)
    finish(send_back, recv_back, sems_back, own_back)

    def unpack_back(k, carry):
        at = pl.multiple_of(k * 8 * NB_BACK, 8 * NB_BACK)
        block = recv_back[pl.ds(k * 8, 8)].astype(F32)
        stage[pl.ds(at, 8 * NB_BACK), :] = block.reshape(8 * NB_BACK, 128)
        return carry

    lax.fori_loop(0, OWNERS // 8, unpack_back, 0)
    for k in range(MOST):
        for n in range(CHUNKS):
            normed[k * OWNERS : (k + 1) * OWNERS, n * 128 : (n + 1) * 128] = stage[
                pl.ds(k * CHUNKS + n, OWNERS, stride=NB_BACK), :
            ].astype(BF16)

    def take(n, carry):
        at = pl.multiple_of(n * 256, 256)
        qkv[0:ROWS, pl.ds(0, 256)] = dot(gather[...], normed[:, pl.ds(at, 256)]).astype(BF16)
        partial = qkv[0:ROWS, pl.ds(0, 256)]
        for m in range(4):
            to = slice(m * 256, (m + 1) * 256)
            hidden[:, to] = hidden[:, to] + dot(partial, w_out[n, :, to])
        return carry

    hidden[...] = embedded[...].astype(F32)
    lax.fori_loop(0, 4, take, 0)
    values = hidden[...]
    mean = jnp.sum(values * values, axis=1, keepdims=True) * (1.0 / D)
    normed[0:ROWS, :] = (values * lax.rsqrt(mean + EPS) * norm_mlp_ref[...]).astype(BF16)
    total[...] = hidden[...]

    def mlp(step, carry):
        which = shard(step)
        for i in range(3):
            at_step(step, i + 1, (ready, 2, i), (ready, 3, i))

        def widen(n, carry):
            at = pl.multiple_of(n * 1024, 1024)
            up = dot(normed[0:ROWS, :], w_up[which, :, pl.ds(at, 1024)])
            normed[ROWS:SLOTS, pl.ds(at, 1024)] = jax.nn.gelu(up).astype(BF16)
            return carry

        lax.fori_loop(0, 1, widen, 0)

        def narrow(n, carry):
            at = pl.multiple_of(n * 1024, 1024)
            total[:, pl.ds(at, 1024)] = total[:, pl.ds(at, 1024)] + dot(
                normed[ROWS:SLOTS, :], w_down[which, :, pl.ds(at, 1024)]
            )
            return carry

        lax.fori_loop(0, 1, narrow, 0)
        return carry

    lax.fori_loop(0, 4, mlp, 0)
    out_ref[...] = total[...].astype(BF16)
    for w in range(4):
        for slot in slots_of(w):
            copy_of(w, slot).wait_send()


def local(
    patches, fields, route, frame, embed, norm_attn, attn_in, attn_out, norm_mlp, mlp_in, mlp_out
):
    by_field = jnp.transpose(patches, (1, 0, 2))
    whole = pl.BlockSpec(memory_space=pl.ANY)
    vmem = pl.BlockSpec(memory_space=pltpu.VMEM)
    return pl.pallas_call(
        kernel,
        out_shape=jax.ShapeDtypeStruct((ROWS, D), BF16),
        in_specs=[whole, whole, vmem, vmem, vmem, vmem, vmem, whole, whole, whole, whole],
        out_specs=vmem,
        scratch_shapes=[
            pltpu.VMEM((4, D, 768), BF16),
            pltpu.VMEM((4, 256, D), BF16),
            pltpu.VMEM((4, D, D), BF16),
            pltpu.VMEM((4, D, D), BF16),
            pltpu.VMEM((D, 768), BF16),
            pltpu.VMEM((FIELDS, PATCH, D), BF16),
            pltpu.VMEM((FIELDS, ROWS, PATCH), BF16),
            pltpu.VMEM((ROWS, D), BF16),
            pltpu.VMEM((OWNERS * NB_OUT, 128), F32),
            pltpu.VMEM((OWNERS, NB_OUT, 128), BF16),
            pltpu.VMEM((OWNERS, NB_OUT, 128), BF16),
            pltpu.VMEM((OWNERS, NB_BACK, 128), BF16),
            pltpu.VMEM((OWNERS, NB_BACK, 128), BF16),
            pltpu.VMEM((SLOTS, D), F32),
            pltpu.VMEM((SLOTS, D), BF16),
            pltpu.VMEM((SLOTS, 768), BF16),
            pltpu.VMEM((ROWS, D), F32),
            pltpu.VMEM((ROWS, D), F32),
            pltpu.VMEM((ROWS, SLOTS), BF16),
            pltpu.SemaphoreType.DMA((6,)),
            pltpu.SemaphoreType.DMA((6,)),
            pltpu.SemaphoreType.DMA((4 * PER_WEIGHT,)),
            pltpu.SemaphoreType.DMA((4 * PER_WEIGHT,)),
            pltpu.SemaphoreType.REGULAR((3,)),
        ],
        compiler_params=pltpu.CompilerParams(
            collective_id=0, has_side_effects=True, vmem_limit_bytes=62 * 1024 * 1024
        ),
        cost_estimate=pl.CostEstimate(
            flops=25_000_000_000, bytes_accessed=16_000_000, transcendentals=11_000_000
        ),
    )(
        by_field,
        embed,
        route,
        frame,
        fields,
        norm_attn.reshape(1, D),
        norm_mlp.reshape(1, D),
        attn_in,
        attn_out,
        mlp_in,
        mlp_out,
    )


def solution(mesh):
    return jax.shard_map(
        local,
        mesh=mesh,
        in_specs=(
            P(("loader", "pack"), None, None),
            P(("loader", "pack")),
            P(("loader", "pack")),
            P(("loader", "pack")),
            P(),
            P(),
            P(None, "pack"),
            P("pack", None),
            P(),
            P(None, "pack"),
            P("pack", None),
        ),
        out_specs=P(("loader", "pack"), None),
        check_vma=False,
    )
```

```python
import functools

import jax
import jax.numpy as jnp
from jax import lax
from jax.experimental import pallas as pl
from jax.experimental.pallas import tpu as pltpu
from jax.sharding import PartitionSpec as P

D = 1024
FIELDS = 11
PATCH = 256
ROWS = 384
OWNERS = 128
MOST = 6
SLOTS = 768
CHUNKS = D // 128
NB_OUT = 56
NB_BACK = 48
EPS = 1e-06
BIG = 1e30
EXP_SCALE = 1.4426950408889634 / 8.0
MESH = pl.DeviceIdType.MESH
F32 = jnp.float32
BF16 = jnp.bfloat16

PER_WEIGHT = 23
WIDE = (3,)


def device(x, y, c, z):
    return (((x % 4) * 4 + y % 4) * 2 + c % 2, z % 4)


def dot(a, b):
    return jnp.dot(a, b, preferred_element_type=F32)


def iota(shape, dim):
    return lax.broadcasted_iota(jnp.int32, shape, dim)


def kernel(
    patches_ref,
    embed_ref,
    route_ref,
    frame_ref,
    fields_ref,
    norm_attn_ref,
    norm_mlp_ref,
    attn_in_ref,
    attn_out_ref,
    mlp_in_ref,
    mlp_out_ref,
    out_ref,
    w_in,
    w_out,
    w_up,
    w_down,
    raw_in,
    embed_v,
    flat,
    embedded,
    stage,
    send_out,
    recv_out,
    send_back,
    recv_back,
    rows,
    normed,
    qkv,
    hidden,
    total,
    gather,
    local_sem,
    row_sem,
    wsend,
    wrecv,
    here,
):
    loader = lax.axis_index("loader")
    z = lax.axis_index("pack")
    x, y, c = loader // 8, (loader // 2) % 4, loader % 2
    me = loader * 4 + z
    r = jnp.where(c == 0, x, y)

    loads = []

    def load(src, dst):
        copy = pltpu.make_async_copy(src, dst, local_sem.at[len(loads)])
        copy.start()
        loads.append(copy)
        return copy

    get_in = load(attn_in_ref, raw_in)
    get_embed = load(embed_ref, embed_v)
    get_patches = load(patches_ref, flat)
    get_out = load(attn_out_ref, w_out.at[z])
    get_up = load(mlp_in_ref, w_up.at[z])
    get_down = load(mlp_out_ref, w_down.at[z])

    def peer(k):
        dx, dc = k % 4, (k // 64 + k) % 2
        dy, dz = (k // 4 + dx) % 4, (k // 16 + 4 - dx) % 4
        px, py, pc, pz = (x + dx) % 4, (y + dy) % 4, (c + dc) % 2, (z + dz) % 4
        to = (px * 4 + py) * 2 + pc
        return (to, pz), to * 4 + pz

    barrier = pltpu.get_barrier_semaphore()
    line_x = [device(x + k, y, c, z) for k in (1, 3, 2)]
    line_y = [device(x, y + k, c, z) for k in (1, 3, 2)]
    line_z = [device(x, y, c, z + k) for k in (1, 3, 2)]
    for to in line_x + line_y + line_z + [device(x, y, c + 1, z)]:
        pl.semaphore_signal(barrier, inc=1, device_id=to, device_id_type=MESH)

    def greet(line, stage):
        for to in line:
            pl.semaphore_signal(here.at[stage], inc=1, device_id=to, device_id_type=MESH)

    def heard(stage):
        pl.semaphore_wait(here.at[stage], 3)

    get_in.wait()

    def reorder(n, carry):
        col = iota((768, 256), 1)
        source = (col >> 6) * 192 + n * 64 + (col & 63)
        pick = (iota((768, 256), 0) == source).astype(BF16)
        at = pl.multiple_of(n * 256, 256)
        w_in[z, :, pl.ds(at, 256)] = dot(raw_in[...], pick).astype(BF16)
        return carry

    lax.fori_loop(0, 3, reorder, 0)

    weights = (w_in, w_out, w_up, w_down)
    z_of = ((z + 3) % 4, (z + 1) % 4, (z + 2) % 4)
    up_z, down_z = device(x, y, c, z + 1), device(x, y, c, z + 3)
    one = jnp.where(c == 0, 1, 0)
    up_r = device(x + one, y + 1 - one, c, z)
    down_r = device(x + 3 * one, y + 3 - 3 * one, c, z)
    other = device(x, y, c + 1, z)

    def part(w, which, q, half=None):
        size = weights[w].shape[1] // 8
        start = (c * 4 + q % 4) * size
        if half is not None:
            size = size // 2
            start = start + half * size
        return weights[w].at[which, pl.ds(pl.multiple_of(start, size), size)]

    def copy_of(w, slot):
        if slot < 2:
            block, to = part(w, z, r), (up_z, down_z)[slot]
        elif slot < 4:
            block, to = part(w, z_of[slot - 2], r, slot - 2), (up_z, down_z)[slot - 2]
        elif slot < 16:
            i, step = (slot - 4) // 4, (slot - 4) % 4
            to = (up_r, down_r)[step % 2]
            if step < 2:
                block = part(w, z_of[i], r)
            else:
                block = part(w, z_of[i], r + (3 if step == 2 else 1), step - 2)
        elif slot < 19:
            size = weights[w].shape[1] // 2
            at = pl.multiple_of(c * size, size)
            block, to = weights[w].at[z_of[slot - 16], pl.ds(at, size)], other
        elif slot < 21:
            block, to = part(w, z, r + 2), (up_z, down_z)[slot - 19]
        else:
            block, to = part(w, z_of[slot - 21], r + 2, slot - 21), (up_z, down_z)[slot - 21]
        return pltpu.make_async_remote_copy(
            block,
            block,
            wsend.at[w * PER_WEIGHT + slot],
            wrecv.at[w * PER_WEIGHT + slot],
            device_id=to,
            device_id_type=MESH,
        )

    def send(w, slot):
        copy_of(w, slot).start()

    def arrived(w, slot):
        copy_of(w, slot).wait_recv()

    def slots_of(w):
        if w in WIDE:
            return [k for k in range(PER_WEIGHT) if k < 4 or k >= 16 or k % 4 < 2]
        return range(19)

    def begin(w):
        send(w, 0)
        send(w, 1)
        if w in WIDE:
            send(w, 19)
            send(w, 20)

    def ring(w, i):
        send(w, 4 + 4 * i)
        send(w, 5 + 4 * i)

    def near(w):
        arrived(w, 0)
        send(w, 2)
        ring(w, 0)
        arrived(w, 1)
        send(w, 3)
        ring(w, 1)
        if w in WIDE:
            arrived(w, 19)
            send(w, 21)
            arrived(w, 20)
            send(w, 22)

    def far(w):
        arrived(w, 2)
        arrived(w, 3)
        ring(w, 2)
        if w in WIDE:
            arrived(w, 21)
            arrived(w, 22)

    def onward(w, i):
        if w in WIDE:
            return
        arrived(w, 4 + 4 * i)
        send(w, 6 + 4 * i)
        arrived(w, 5 + 4 * i)
        send(w, 7 + 4 * i)

    def share(w, i):
        last = 4 if w in WIDE else 6
        arrived(w, last + 4 * i)
        arrived(w, last + 1 + 4 * i)
        send(w, 16 + i)

    def ready(w, i):
        arrived(w, 16 + i)

    pl.semaphore_wait(barrier, 10)
    begin(0)
    greet(line_z, 0)
    get_out.wait()

    route_row = route_ref[...].reshape(1, ROWS)
    frame_row = frame_ref[...].reshape(1, ROWS).astype(F32)
    eye = iota((ROWS, ROWS), 0) == iota((ROWS, ROWS), 1)

    def column(row):
        return jnp.sum(jnp.where(eye, row, 0.0), axis=1, keepdims=True)

    onehot = (iota((OWNERS, ROWS), 0) == route_row).astype(F32)
    before = (iota((ROWS, ROWS), 0) < iota((ROWS, ROWS), 1)).astype(BF16)
    rank_row = jnp.sum(dot(onehot.astype(BF16), before) * onehot, axis=0, keepdims=True)
    heard(0)
    fields_col = column(fields_ref[...].reshape(1, ROWS).astype(F32))
    greet(line_y, 1)

    get_embed.wait()
    get_patches.wait()
    for f in range(FIELDS):
        pixels = flat[f]
        flat[f] = jnp.where(fields_col > float(f), pixels.astype(F32), 0.0).astype(BF16)

    def embed_tile(n, carry):
        at = pl.multiple_of(n * 1024, 1024)
        acc = dot(flat[0], embed_v[0, :, pl.ds(at, 1024)])
        for f in range(1, FIELDS):
            acc = acc + dot(flat[f], embed_v[f, :, pl.ds(at, 1024)])
        embedded[:, pl.ds(at, 1024)] = acc.astype(BF16)
        return carry

    lax.fori_loop(0, 1, embed_tile, 0)

    heard(1)
    greet(line_x, 2)
    near(0)

    for k in range(MOST):
        place = onehot * (rank_row == float(k)).astype(F32)
        tag = jnp.sum(place * (frame_row + 1.0), axis=1, keepdims=True) - 1.0
        placed = dot(place.astype(BF16), embedded[...])
        for n in range(CHUNKS):
            stage[pl.ds(k * CHUNKS + n, OWNERS, stride=NB_OUT), :] = placed[
                :, n * 128 : (n + 1) * 128
            ]
        stage[pl.ds(48 + k, OWNERS, stride=NB_OUT), :] = jnp.broadcast_to(tag, (OWNERS, 128))
    for k in range(48 + MOST, NB_OUT):
        stage[pl.ds(k, OWNERS, stride=NB_OUT), :] = jnp.zeros((OWNERS, 128), F32)

    def pack_out(k, carry):
        at = pl.multiple_of(k * 8 * NB_OUT, 8 * NB_OUT)
        block = stage[pl.ds(at, 8 * NB_OUT), :]
        send_out[pl.ds(k * 8, 8)] = block.reshape(8, NB_OUT, 128).astype(BF16)
        return carry

    lax.fori_loop(0, OWNERS // 8, pack_out, 0)

    heard(2)

    def exchange(source, target, sems):
        own = pltpu.make_async_copy(source.at[me], target.at[me], sems[2])
        own.start()

        def one_peer(k, carry):
            to, index = peer(k)
            pltpu.make_async_remote_copy(
                source.at[index],
                target.at[me],
                sems[0],
                sems[1],
                device_id=to,
                device_id_type=MESH,
            ).start()
            return carry

        lax.fori_loop(1, OWNERS, one_peer, 0)
        return own

    def finish(source, target, sems, own):
        own.wait()
        pltpu.make_async_remote_copy(
            source.at[pl.ds(0, OWNERS - 1)],
            target.at[pl.ds(0, OWNERS - 1)],
            sems[0],
            sems[1],
            device_id=other,
            device_id_type=MESH,
        ).wait()

    sems_out = (row_sem.at[0], row_sem.at[1], row_sem.at[2])
    sems_back = (row_sem.at[3], row_sem.at[4], row_sem.at[5])

    own_out = exchange(send_out, recv_out, sems_out)
    route_col = column(route_row.astype(F32))
    rank_col = column(rank_row)
    owner_lane = iota((ROWS, OWNERS), 1).astype(F32)
    for k in range(MOST):
        gather[:, k * OWNERS : (k + 1) * OWNERS] = (
            (owner_lane == route_col) & (rank_col == float(k))
        ).astype(BF16)
    begin(1)
    get_up.wait()
    get_down.wait()
    begin(2)
    far(0)
    onward(0, 0)
    onward(0, 1)
    onward(0, 2)
    share(0, 0)
    share(0, 1)
    share(0, 2)
    finish(send_out, recv_out, sems_out, own_out)

    def unpack_out(k, carry):
        at = pl.multiple_of(k * 8 * NB_OUT, 8 * NB_OUT)
        block = recv_out[pl.ds(k * 8, 8)].astype(F32)
        stage[pl.ds(at, 8 * NB_OUT), :] = block.reshape(8 * NB_OUT, 128)
        return carry

    lax.fori_loop(0, OWNERS // 8, unpack_out, 0)

    def norm_rows(k, carry):
        at = pl.multiple_of(k * OWNERS, OWNERS)
        square = jnp.zeros((OWNERS, 128), F32)
        for n in range(CHUNKS):
            part_rows = stage[pl.ds(k * CHUNKS + n, OWNERS, stride=NB_OUT), :]
            rows[pl.ds(at, OWNERS), n * 128 : (n + 1) * 128] = part_rows
            square = square + part_rows * part_rows
        mean = jnp.sum(square, axis=1, keepdims=True) * (1.0 / D)
        scaled = rows[pl.ds(at, OWNERS), :] * lax.rsqrt(mean + EPS) * norm_attn_ref[...]
        normed[pl.ds(at, OWNERS), :] = scaled.astype(BF16)
        return carry

    for k in range(MOST):
        norm_rows(k, 0)

    tags = jnp.concatenate(
        [stage[pl.ds(48 + k, OWNERS, stride=NB_OUT), :] for k in range(MOST)], axis=0
    )
    lane = iota((SLOTS, 128), 1)
    low = lane < 64
    same_tag = tags == ((lane & 63) - 1).astype(F32)
    tag_query = same_tag.astype(BF16)
    tag_key = jnp.where(same_tag | ((lane & 63) > 4), 0.0, -BIG).astype(BF16)

    def shard(step):
        which = jnp.where(step == 1, z_of[0], jnp.where(step == 2, z_of[1], z_of[2]))
        return jnp.where(step == 0, z, which)

    def at_step(step, now, *actions):
        @pl.when(step == now)
        def _():
            for action, *given in actions:
                action(*given)

    def attend(step, carry):
        which = shard(step)
        for i in range(3):
            at_step(step, i + 1, (ready, 0, i))

        def project(n, carry):
            at = pl.multiple_of(n * 768, 768)
            qkv[:, pl.ds(at, 768)] = dot(normed[...], w_in[which, :, pl.ds(at, 768)]).astype(BF16)
            return carry

        lax.fori_loop(0, 1, project, 0)

        def pair(p, carry):
            at = pl.multiple_of(p * 128, 128)
            query = qkv[:, pl.ds(at, 128)]
            key = qkv[:, pl.ds(at + 256, 128)]
            value = qkv[:, pl.ds(at + 512, 128)]
            results = []
            for h in range(2):
                mine = low if h == 0 else jnp.logical_not(low)
                keys = jnp.where(mine, key, tag_key)
                values = jnp.where(mine, value, jnp.ones_like(value))
                queries = jnp.where(mine, query, tag_query)
                blocks = []
                for b in range(2):
                    scores = lax.dot_general(
                        queries[b * 384 : (b + 1) * 384],
                        keys,
                        (((1,), (1,)), ((), ())),
                        preferred_element_type=F32,
                    )
                    highest = jnp.max(scores, axis=1, keepdims=True)
                    shifted = jnp.exp2((scores - highest) * EXP_SCALE).astype(BF16)
                    blocks.append(dot(shifted, values))
                results.append(blocks)
            for b in range(2):
                half = low[:384]
                top = jnp.where(half, results[0][b], results[1][b])
                sums = jnp.where(half, results[1][b], results[0][b])
                result = top / pltpu.roll(sums, 64, 1)
                for k in range(3):
                    first = (b * 3 + k) * CHUNKS + which * 2 + p
                    stage[pl.ds(first, OWNERS, stride=NB_BACK), :] = result[
                        k * OWNERS : (k + 1) * OWNERS
                    ]
            for now in range(8):
                at_step(step * 2 + p, now, *schedule[now])
            return carry

        lax.fori_loop(0, 2, pair, 0)
        return carry

    schedule = (
        [(near, 1), (near, 2), (begin, 3)],
        [(far, 1), (far, 2)],
        [(onward, 1, 0), (onward, 1, 1), (onward, 1, 2), (onward, 2, 0)],
        [(onward, 2, 1), (near, 3)],
        [(onward, 2, 2), (share, 1, 0), (share, 1, 1), (share, 1, 2)],
        [(far, 3)],
        [(share, 2, 0), (share, 2, 1), (share, 2, 2)],
        [],
    )
    lax.fori_loop(0, 4, attend, 0)

    def pack_back(k, carry):
        at = pl.multiple_of(k * 8 * NB_BACK, 8 * NB_BACK)
        block = stage[pl.ds(at, 8 * NB_BACK), :]
        send_back[pl.ds(k * 8, 8)] = block.reshape(8, NB_BACK, 128).astype(BF16)
        return carry

    lax.fori_loop(0, OWNERS // 8, pack_back, 0)
    own_back = exchange(send_back, recv_back, sems_back)
    for i in range(3):
        share(3, i)
    for i in range(3):
        ready(1, i)
    finish(send_back, recv_back, sems_back, own_back)

    def unpack_back(k, carry):
        at = pl.multiple_of(k * 8 * NB_BACK, 8 * NB_BACK)
        block = recv_back[pl.ds(k * 8, 8)].astype(F32)
        stage[pl.ds(at, 8 * NB_BACK), :] = block.reshape(8 * NB_BACK, 128)
        return carry

    lax.fori_loop(0, OWNERS // 8, unpack_back, 0)
    for k in range(MOST):
        for n in range(CHUNKS):
            normed[k * OWNERS : (k + 1) * OWNERS, n * 128 : (n + 1) * 128] = stage[
                pl.ds(k * CHUNKS + n, OWNERS, stride=NB_BACK), :
            ].astype(BF16)

    def take(n, carry):
        at = pl.multiple_of(n * 256, 256)
        qkv[0:ROWS, pl.ds(0, 256)] = dot(gather[...], normed[:, pl.ds(at, 256)]).astype(BF16)
        partial = qkv[0:ROWS, pl.ds(0, 256)]
        for m in range(4):
            to = slice(m * 256, (m + 1) * 256)
            hidden[:, to] = hidden[:, to] + dot(partial, w_out[n, :, to])
        return carry

    hidden[...] = embedded[...].astype(F32)
    lax.fori_loop(0, 4, take, 0)
    values = hidden[...]
    mean = jnp.sum(values * values, axis=1, keepdims=True) * (1.0 / D)
    normed[0:ROWS, :] = (values * lax.rsqrt(mean + EPS) * norm_mlp_ref[...]).astype(BF16)
    total[...] = hidden[...]

    def mlp(step, carry):
        which = shard(step)
        for i in range(3):
            at_step(step, i + 1, (ready, 2, i), (ready, 3, i))

        def widen(n, carry):
            at = pl.multiple_of(n * 1024, 1024)
            up = dot(normed[0:ROWS, :], w_up[which, :, pl.ds(at, 1024)])
            normed[ROWS:SLOTS, pl.ds(at, 1024)] = jax.nn.gelu(up).astype(BF16)
            return carry

        lax.fori_loop(0, 1, widen, 0)

        def narrow(n, carry):
            at = pl.multiple_of(n * 1024, 1024)
            total[:, pl.ds(at, 1024)] = total[:, pl.ds(at, 1024)] + dot(
                normed[ROWS:SLOTS, :], w_down[which, :, pl.ds(at, 1024)]
            )
            return carry

        lax.fori_loop(0, 1, narrow, 0)
        return carry

    lax.fori_loop(0, 4, mlp, 0)
    out_ref[...] = total[...].astype(BF16)
    for w in range(4):
        for slot in slots_of(w):
            copy_of(w, slot).wait_send()


def local(
    patches, fields, route, frame, embed, norm_attn, attn_in, attn_out, norm_mlp, mlp_in, mlp_out
):
    by_field = jnp.transpose(patches, (1, 0, 2))
    whole = pl.BlockSpec(memory_space=pl.ANY)
    vmem = pl.BlockSpec(memory_space=pltpu.VMEM)
    return pl.pallas_call(
        kernel,
        out_shape=jax.ShapeDtypeStruct((ROWS, D), BF16),
        in_specs=[whole, whole, vmem, vmem, vmem, vmem, vmem, whole, whole, whole, whole],
        out_specs=vmem,
        scratch_shapes=[
            pltpu.VMEM((4, D, 768), BF16),
            pltpu.VMEM((4, 256, D), BF16),
            pltpu.VMEM((4, D, D), BF16),
            pltpu.VMEM((4, D, D), BF16),
            pltpu.VMEM((D, 768), BF16),
            pltpu.VMEM((FIELDS, PATCH, D), BF16),
            pltpu.VMEM((FIELDS, ROWS, PATCH), BF16),
            pltpu.VMEM((ROWS, D), BF16),
            pltpu.VMEM((OWNERS * NB_OUT, 128), F32),
            pltpu.VMEM((OWNERS, NB_OUT, 128), BF16),
            pltpu.VMEM((OWNERS, NB_OUT, 128), BF16),
            pltpu.VMEM((OWNERS, NB_BACK, 128), BF16),
            pltpu.VMEM((OWNERS, NB_BACK, 128), BF16),
            pltpu.VMEM((SLOTS, D), F32),
            pltpu.VMEM((SLOTS, D), BF16),
            pltpu.VMEM((SLOTS, 768), BF16),
            pltpu.VMEM((ROWS, D), F32),
            pltpu.VMEM((ROWS, D), F32),
            pltpu.VMEM((ROWS, SLOTS), BF16),
            pltpu.SemaphoreType.DMA((6,)),
            pltpu.SemaphoreType.DMA((6,)),
            pltpu.SemaphoreType.DMA((4 * PER_WEIGHT,)),
            pltpu.SemaphoreType.DMA((4 * PER_WEIGHT,)),
            pltpu.SemaphoreType.REGULAR((3,)),
        ],
        compiler_params=pltpu.CompilerParams(
            collective_id=0, has_side_effects=True, vmem_limit_bytes=62 * 1024 * 1024
        ),
        cost_estimate=pl.CostEstimate(
            flops=25_000_000_000, bytes_accessed=16_000_000, transcendentals=11_000_000
        ),
    )(
        by_field,
        embed,
        route,
        frame,
        fields,
        norm_attn.reshape(1, D),
        norm_mlp.reshape(1, D),
        attn_in,
        attn_out,
        mlp_in,
        mlp_out,
    )


def solution(mesh):
    return jax.shard_map(
        local,
        mesh=mesh,
        in_specs=(
            P(("loader", "pack"), None, None),
            P(("loader", "pack")),
            P(("loader", "pack")),
            P(("loader", "pack")),
            P(),
            P(),
            P(None, "pack"),
            P("pack", None),
            P(),
            P(None, "pack"),
            P("pack", None),
        ),
        out_specs=P(("loader", "pack"), None),
        check_vma=False,
    )
```
